512 devices in a mesh: tile: 16 (over z_lo, core), wide: 32 (over y, z_hi, x).
Axes of the slice: x: 4, y: 4, z: 16 (z_hi: 2, z_lo: 8; z = z_hi * 8 + z_lo), core: 2. Of those that a mesh axis runs over, the one named last changes fastest.
Arguments:
- coefficients: bfloat16 [1536, 1536], P('tile', 'wide'), may hold values from -6 to 6
- integrals: bfloat16 [400, 400], replicated, may hold values from -0.0390625 to 0.0390625
- targets: int32 [110, 1536], replicated, may hold values from 0 to 1535, as said below
- orbital_pairs: int32 [110, 1536], replicated, may hold values from 0 to 399, as said below
- phases: int32 [110, 1536], replicated, may hold values from -1 to 1, as said below
Outputs:
- sigma: float32 [1536, 1536], P('tile', 'wide')
The draws below stay inside these ranges and needn't reach their ends.
Inputs may be any that keep to these rules, and one draw needn't show every extreme that they name: targets[e, b] is the string that excitation e of string b leads to; the entries e = k * (11) are b itself. `orbital_pairs`: each column holds 110 distinct pairs p * 20 + q, q one of the string's 10 occupied orbitals and p either q or an empty orbital. `phases`: each entry is 1 or -1; 1 where the target is the string itself.
All inputs are finite; a program needn't handle non-finite values.
Results may differ from the reference program's by a relative error of at most 0.0029.
Values may be sent and summed in bfloat16 or wider, within the bound.
A program may use at most 64 MiB of HBM per device.

```python
import math
import jax
import jax.numpy as jnp
from jax import lax

NORB = 20
NOCC = 10
NPQ = 400
NEXC = 110
NS = 1536


def string_tables(key):
    vacant_count = NORB - NOCC
    scores = jax.random.randint(jax.random.fold_in(key, 11), (NS, NORB), 0, 1 << 20)
    scores = scores * NORB + jnp.arange(NORB, dtype=jnp.int32)[None]
    order = jnp.argsort(scores, axis=1, stable=True).astype(jnp.int32)
    occupied = order[:, :NOCC]
    vacant = order[:, NOCC:]
    creators = jnp.concatenate([occupied[:, :, None], jnp.broadcast_to(vacant[:, None, :], (NS, NOCC, vacant_count))], axis=2)
    pair_rows = (creators * NORB + occupied[:, :, None]).reshape(NS, NEXC)
    diagonal = jnp.broadcast_to((jnp.arange(vacant_count + 1) == 0)[None, None, :], (NS, NOCC, vacant_count + 1)).reshape(NS, NEXC)
    random_targets = jax.random.randint(jax.random.fold_in(key, 12), (NS, NEXC), 0, NS)
    selves = jnp.broadcast_to(jnp.arange(NS, dtype=jnp.int32)[:, None], (NS, NEXC))
    target_rows = jnp.where(diagonal, selves, random_targets).astype(jnp.int32)
    random_signs = jax.random.randint(jax.random.fold_in(key, 13), (NS, NEXC), 0, 2) * 2 - 1
    sign_rows = jnp.where(diagonal, 1, random_signs).astype(jnp.int32)
    return (target_rows.T, pair_rows.T, sign_rows.T)


def draw_targets(key, part):
    return string_tables(key)[0]


def draw_orbital_pairs(key, part):
    return string_tables(key)[1]


def draw_phases(key, part):
    return string_tables(key)[2]


def steps_of(key, extent, split, low, largest):
    factor_of = 1.0
    for position, blocks in split:
        steps = jax.random.uniform(jax.random.fold_in(jax.random.fold_in(key, 6), position), (blocks,), jnp.float32, low / len(split), largest / len(split))
        factor_of = factor_of * jnp.repeat(jnp.exp(steps), extent[position] // blocks).reshape((-1,) + (1,) * (len(extent) - 1 - position))
    return factor_of


def noise(own_key, extent, deviation, bound, shards=(), held_as=jnp.bfloat16):
    entries = deviation * jax.random.normal(own_key, extent, jnp.float32)
    if shards:
        entries = entries * steps_of(own_key, extent, shards, -0.22, 0.18)
    return jnp.clip(entries, -bound, bound).astype(held_as)


def setup_inputs(seed: int = 0) -> dict:
    key_list = jax.random.split(jax.random.key(seed), 6)
    return {
        "coefficients": noise(key_list[0], (NS, NS), 1.0, 6.0, ((0, 16), (1, 32))),
        "integrals": noise(key_list[1], (NPQ, NPQ), (2 * NEXC * NEXC) ** -0.5, 0.0390625),
        "targets": draw_targets(jax.random.fold_in(key_list[5], 71), 0),
        "orbital_pairs": draw_orbital_pairs(jax.random.fold_in(key_list[5], 71), 0),
        "phases": draw_phases(jax.random.fold_in(key_list[5], 71), 0),
    }


def one_side(source, targets, orbital_pairs, phases, integrals):
    total = source.shape[1]
    rows = source.shape[0]
    npairs = integrals.shape[0]
    blocked = math.gcd(rows, 64)
    sign_table = phases.astype(jnp.float32)
    coupling = integrals.astype(jnp.float32)
    string_index = jnp.arange(total, dtype=jnp.int32)[:, None]

    def block_part(group_rows):
        values = group_rows.astype(jnp.float32)[:, targets] * sign_table[None]
        spread = jnp.zeros((blocked, total, npairs), jnp.float32)
        spread = spread.at[:, string_index, orbital_pairs].set(values)
        spread = lax.optimization_barrier(spread.astype(jnp.bfloat16)).astype(jnp.float32)
        coupled = jnp.einsum("abq,pq->abp", spread, coupling)
        coupled = lax.optimization_barrier(coupled.astype(jnp.bfloat16)).astype(jnp.float32)
        picked = jnp.take_along_axis(coupled, orbital_pairs[None], axis=2) * sign_table[None]
        result = jnp.zeros((blocked, total), jnp.float32)
        return result.at[:, targets].add(picked)

    parts = lax.map(block_part, source.reshape(rows // blocked, blocked, total))
    return parts.reshape(rows, total)


def reference(coefficients, integrals, targets, orbital_pairs, phases):
    string_targets = targets.T
    string_pairs = orbital_pairs.T
    string_phases = phases.T
    beta_part = one_side(coefficients, string_targets, string_pairs, string_phases, integrals)
    alpha_part = one_side(coefficients.T, string_targets, string_pairs, string_phases, integrals).T
    return beta_part + alpha_part
```

```python
import functools
import types

import jax
import jax.numpy as jnp
from jax import lax
from jax.experimental import pallas as pl
from jax.experimental.pallas import tpu as pltpu
from jax.sharding import PartitionSpec as P

LANES = 128
MESH = pl.DeviceIdType.MESH


def plan_of(mesh, coef_shape, exc_shape, pair_count):
    tiles, wides = mesh.shape["tile"], mesh.shape["wide"]
    xs = 4 if wides == 32 else 2
    ys = wides // (2 * xs)
    strings = coef_shape[0]
    rows, cols = strings // tiles, strings // wides
    chunks = tiles // 4
    chunk = cols // chunks
    return types.SimpleNamespace(
        tiles=tiles,
        wides=wides,
        xs=xs,
        ys=ys,
        plane=xs * ys * 2,
        strings=strings,
        rows=rows,
        cols=cols,
        quad=tiles // 4,
        chunks=chunks,
        chunk=chunk,
        chunk_pad=-(-chunk // 16) * 16,
        sets=xs * ys // 2,
        own=strings // (xs * ys * 2),
        exc=exc_shape[0],
        pairs=pair_count,
        pair_pad=-(-pair_count // LANES) * LANES,
        step=8,
    )


def kernel(n, coef, integ, tgt, prs, phs, out, raw, tabs, g_pad, c_pad, first, hold, gath, xt, x_all,
           t_all, w_all, u_all, part, rs_out, rs_in, fin, fin_in, s_tab, s1, r1, s2, r2, s3, r3, s4, r4):
    bf16, f32 = jnp.bfloat16, jnp.float32
    slot_rows = n.cols + n.quad * n.chunk_pad
    tile, wide = lax.axis_index("tile"), lax.axis_index("wide")
    core, zl = lax.rem(tile, 2), tile // 2
    x, zh, y = lax.rem(wide, n.xs), lax.rem(wide // n.xs, 2), wide // (2 * n.xs)
    me = (y * n.xs + x) * 2 + core

    def device(xx, yy, zzh, zzl, cc):
        return (zzl * 2 + cc, (yy * 2 + zzh) * n.xs + xx)

    def plane_device(p):
        return device(lax.rem(p // 2, n.xs), p // (2 * n.xs), zh, zl, lax.rem(p, 2))

    def peer(d):
        return lax.rem(me + d, n.plane)

    def source(d):
        return lax.rem(me + n.plane - d, n.plane)

    def flip(a, b):
        return lax.rem(a + b, 2)

    crosses = zh != core
    far = device(x, y, 1 - zh, zl, 1 - core)
    my_quad, my_slot = tile // n.quad, lax.rem(tile, n.quad)
    to_x = (x // 2) * 2 + flip(lax.rem(x, 2), my_quad // 2)
    to_core = lax.rem(my_quad, 2)

    def target(m):
        zz = 2 * m + lax.rem(x, 2)
        is_me = (to_x == x) & (to_core == core) & (zz == zl)
        return device(to_x, y, zh, zz, to_core), is_me

    from_x = (x // 2) * 2 + lax.rem(zl, 2)
    held_quad = 2 * flip(lax.rem(x, 2), lax.rem(zl, 2)) + core

    def giver(k):
        t = held_quad * n.quad + k
        is_me = (from_x == x) & (t == tile)
        return device(from_x, y, zh, t // 2, lax.rem(t, 2)), is_me

    held_chunk = zl // 2

    start = me * n.own
    window = jnp.minimum(start // LANES * LANES, n.strings - 2 * LANES)
    window = pl.multiple_of(window, LANES)
    loads = [
        pltpu.make_async_copy(
            ref.at[:, pl.ds(window, 2 * LANES)], raw.at[i], s_tab.at[i]
        )
        for i, ref in enumerate((tgt, prs, phs))
    ]
    for load in loads:
        load.start()

    barrier = pltpu.get_barrier_semaphore()

    def greet(d, carry):
        pl.semaphore_signal(barrier, inc=1, device_id=plane_device(peer(d)), device_id_type=MESH)
        return carry

    lax.fori_loop(1, n.plane, greet, 0)
    for m in range(n.chunks):
        where_to, is_me = target(m)

        @pl.when(jnp.logical_not(is_me))
        def _():
            pl.semaphore_signal(barrier, inc=1, device_id=where_to, device_id_type=MESH)

    for k in range(n.quad):
        whose, is_me = giver(k)

        @pl.when(jnp.logical_not(is_me))
        def _():
            pl.semaphore_signal(barrier, inc=1, device_id=whose, device_id_type=MESH)

    @pl.when(crosses)
    def _():
        pl.semaphore_signal(barrier, inc=1, device_id=far, device_id_type=MESH)

    c_pad[...] = jnp.zeros_like(c_pad)
    c_pad[0:n.rows, 0:n.cols] = coef[...].astype(f32)
    block_t = c_pad[...].T
    first[0:n.cols] = block_t[0:n.cols].astype(bf16)
    for m in range(n.chunks):
        piece = block_t[m * n.chunk : m * n.chunk + n.chunk_pad]
        at = n.cols + m * n.chunk_pad
        first[at : at + n.chunk_pad] = piece.astype(bf16)

    g_pad[...] = jnp.zeros_like(g_pad)
    g_pad[0:n.pairs, 0:n.pairs] = integ[...]
    tabs[...] = jnp.zeros_like(tabs)
    for load in loads:
        load.wait()
    tabs[:, 0 : n.exc] = raw[...]

    itself = jnp.int32(0)
    for m in range(n.chunks):
        itself = itself + target(m)[1].astype(jnp.int32)
    expected = n.plane - 1 + n.chunks + n.quad - 2 * itself + crosses.astype(jnp.int32)
    pl.semaphore_wait(barrier, expected)

    def piece_rows(k):
        return pl.ds(pl.multiple_of(n.cols + k * n.chunk_pad, 16), n.chunk_pad)

    swap = pltpu.make_async_remote_copy(
        src_ref=first.at[pl.ds(0, n.cols)],
        dst_ref=hold.at[pl.ds(0, n.cols)],
        send_sem=s1.at[0],
        recv_sem=r1.at[0],
        device_id=far,
        device_id_type=MESH,
    )

    def give(m):
        return pltpu.make_async_remote_copy(
            src_ref=first.at[piece_rows(m)],
            dst_ref=hold.at[piece_rows(my_slot)],
            send_sem=s1.at[1 + m],
            recv_sem=r1.at[1 + my_slot],
            device_id=target(m)[0],
            device_id_type=MESH,
        )

    def take(k):
        return pltpu.make_async_remote_copy(
            src_ref=first.at[piece_rows(0)],
            dst_ref=hold.at[piece_rows(k)],
            send_sem=s1.at[1],
            recv_sem=r1.at[1 + k],
            device_id=giver(k)[0],
            device_id_type=MESH,
        )

    @pl.when(crosses)
    def _():
        swap.start()

    @pl.when(jnp.logical_not(crosses))
    def _():
        hold[0 : n.cols] = first[0 : n.cols]

    for m in range(n.chunks):
        is_me = target(m)[1]

        @pl.when(jnp.logical_not(is_me))
        def _():
            give(m).start()

        @pl.when(is_me)
        def _():
            hold[piece_rows(my_slot)] = first[piece_rows(m)]

    offset = start - window
    lane = lax.broadcasted_iota(jnp.int32, (LANES, LANES), 1).astype(f32).astype(bf16)
    one, zero = jnp.ones((), bf16), jnp.zeros((), bf16)

    def spread_col(col):
        return jnp.broadcast_to(col, (LANES, LANES)).astype(bf16)

    def build(it, carry):
        shift = lax.rem(2 * 2 * LANES - offset - it * n.step, 2 * LANES)
        t = pltpu.roll(tabs[0], shift, 1)[:, 0:LANES]
        q = pltpu.roll(tabs[1], shift, 1)[:, 0:LANES]
        s = pltpu.roll(tabs[2], shift, 1)[:, 0:LANES].astype(f32)
        t_hi, t_lo = (t // LANES).astype(f32), lax.rem(t, LANES).astype(f32)
        q_hi, q_lo = (q // LANES).astype(f32), lax.rem(q, LANES).astype(f32)
        for u in range(n.step):
            b = it * n.step + u
            rows = pl.ds(pl.multiple_of(b * LANES, LANES), LANES)
            hi, lo = spread_col(t_hi[:, u : u + 1]), spread_col(t_lo[:, u : u + 1])
            hot = jnp.where(lo == lane, one, zero)
            for kt in range(n.strings // LANES):
                t_all[rows, kt * LANES : (kt + 1) * LANES] = jnp.where(hi == kt, hot, zero)
            hi, lo = spread_col(q_hi[:, u : u + 1]), spread_col(q_lo[:, u : u + 1])
            sign = spread_col(s[:, u : u + 1])
            hot = jnp.where(lo == lane, sign, zero)
            signed = jnp.concatenate(
                [jnp.where(hi == kt, hot, zero) for kt in range(n.pair_pad // LANES)], axis=1
            )
            picked = lax.dot_general(
                signed, g_pad[...], (((1,), (1,)), ((), ())), preferred_element_type=f32
            ).astype(bf16)
            w_all[b] = lax.dot_general(
                picked, signed, (((1,), (1,)), ((), ())), preferred_element_type=f32
            ).astype(bf16)
        return carry

    builds = n.own // n.step
    early = max(1, builds // 3)
    lax.fori_loop(0, early, build, 0)

    @pl.when(crosses)
    def _():
        swap.wait_recv()

    for k in range(n.quad):

        @pl.when(jnp.logical_not(giver(k)[1]))
        def _():
            take(k).wait_recv()

    def share(d, into):
        return pltpu.make_async_remote_copy(
            src_ref=hold,
            dst_ref=gath.at[into],
            send_sem=s2.at[d],
            recv_sem=r2.at[d],
            device_id=plane_device(peer(d)),
            device_id_type=MESH,
        )

    def start_share(d, carry):
        share(d, me).start()
        return carry

    lax.fori_loop(1, n.plane, start_share, 0)
    gath[me] = hold[...]

    lax.fori_loop(early, builds, build, 0)

    def wait_share(d, carry):
        share(d, source(d)).wait_recv()
        return carry

    lax.fori_loop(1, n.plane, wait_share, 0)

    for w in range(n.plane):
        yy, cc, xx = w // (2 * n.xs), w // n.xs % 2, w % n.xs
        p = (yy * n.xs + xx) * 2 + cc
        xt[w * n.cols : (w + 1) * n.cols] = gath[p, 0 : n.cols].astype(f32)
    for kt in range(n.strings // LANES):
        at = slice(kt * LANES, (kt + 1) * LANES)
        x_all[0:LANES, at] = xt[at].T.astype(bf16)

    lane_i = lax.broadcasted_iota(jnp.int32, (LANES, LANES), 1)
    zl_odd = lax.rem(zl, 2)

    def alpha_piece(t):
        quad, slot = t // n.quad, t % n.quad
        at = n.cols + slot * n.chunk_pad
        pieces = []
        for s in range(n.sets):
            yy, xh = s // (n.xs // 2), s % (n.xs // 2)
            xx = 2 * xh + flip(zl_odd, quad // 2)
            p = (yy * n.xs + xx) * 2 + quad % 2
            pieces.append(gath[p, at : at + n.chunk_pad].astype(f32))
        short = LANES - n.sets * n.chunk_pad
        if short:
            pieces.append(jnp.zeros((short, LANES), f32))
        return jnp.concatenate(pieces, axis=0)

    for four in range(n.tiles // 4):
        p0, p1, p2, p3 = (alpha_piece(4 * four + i) for i in range(4))
        p1, p2, p3 = pltpu.roll(p1, 96, 1), pltpu.roll(p2, 64, 1), pltpu.roll(p3, 32, 1)
        tiles3 = (
            jnp.where(lane_i < 96, p0, p1),
            jnp.where(lane_i < 64, p1, p2),
            jnp.where(lane_i < 32, p2, p3),
        )
        for i, value in enumerate(tiles3):
            at = (3 * four + i) * LANES
            x_all[LANES : 2 * LANES, at : at + LANES] = value.astype(bf16)

    def couple(it, carry):
        rows = pl.ds(pl.multiple_of(it * 2 * LANES, 2 * LANES), 2 * LANES)
        v = lax.dot_general(
            x_all[...], t_all[rows, :], (((1,), (1,)), ((), ())), preferred_element_type=f32
        ).astype(bf16)
        for u in range(2):
            value = jnp.dot(
                v[:, u * LANES : (u + 1) * LANES], w_all[it * 2 + u], preferred_element_type=f32
            )
            at = pl.ds(pl.multiple_of((it * 2 + u) * LANES, LANES), LANES)
            u_all[:, at] = value.astype(bf16)
        return carry

    lax.fori_loop(0, n.own // 2, couple, 0)

    width = 3 * LANES

    def scatter(it, carry):
        at = pl.ds(pl.multiple_of(it * width, LANES), width)
        part[:, at] = jnp.dot(u_all[...], t_all[:, at], preferred_element_type=f32)
        return carry

    lax.fori_loop(0, n.strings // width, scatter, 0)

    for kt in range(n.strings // LANES):
        at = slice(kt * LANES, (kt + 1) * LANES)
        xt[at] = part[0:LANES, at].T
    for w in range(n.plane):
        yy, cc, xx = w // (2 * n.xs), w // n.xs % 2, w % n.xs
        p = (yy * n.xs + xx) * 2 + cc
        rs_out[p, 0 : n.cols] = xt[w * n.cols : (w + 1) * n.cols].astype(bf16)
    for four in range(n.tiles // 4):
        t0, t1, t2 = (
            part[LANES : 2 * LANES, (3 * four + i) * LANES : (3 * four + i + 1) * LANES]
            for i in range(3)
        )
        roll = functools.partial(pltpu.roll, axis=1)
        values = (
            t0,
            jnp.where(lane_i < 32, roll(t0, 32), roll(t1, 32)),
            jnp.where(lane_i < 64, roll(t1, 64), roll(t2, 64)),
            roll(t2, 96),
        )
        for i, value in enumerate(values):
            t = 4 * four + i
            quad, slot = t // n.quad, t % n.quad
            at = n.cols + slot * n.chunk_pad
            value = value.astype(bf16)
            for s in range(n.sets):
                yy, xh = s // (n.xs // 2), s % (n.xs // 2)
                xx = 2 * xh + flip(zl_odd, quad // 2)
                p = (yy * n.xs + xx) * 2 + quad % 2
                rs_out[p, at : at + n.chunk_pad] = value[s * n.chunk_pad : (s + 1) * n.chunk_pad]

    def pass_on(d, frm, into):
        return pltpu.make_async_remote_copy(
            src_ref=rs_out.at[frm],
            dst_ref=rs_in.at[into],
            send_sem=s3.at[d],
            recv_sem=r3.at[d],
            device_id=plane_device(peer(d)),
            device_id_type=MESH,
        )

    def start_pass(d, carry):
        pass_on(d, peer(d), me).start()
        return carry

    lax.fori_loop(1, n.plane, start_pass, 0)
    fin[...] = rs_out[me].astype(f32)

    def add_pass(d, carry):
        pass_on(d, peer(d), source(d)).wait_recv()
        fin[...] += rs_in[source(d)].astype(f32)
        return carry

    lax.fori_loop(1, n.plane, add_pass, 0)

    swap_back = pltpu.make_async_remote_copy(
        src_ref=fin.at[pl.ds(0, n.cols)],
        dst_ref=fin_in.at[pl.ds(0, n.cols)],
        send_sem=s4.at[0],
        recv_sem=r4.at[0],
        device_id=far,
        device_id_type=MESH,
    )

    def give_back(k):
        return pltpu.make_async_remote_copy(
            src_ref=fin.at[piece_rows(k)],
            dst_ref=fin_in.at[piece_rows(held_chunk)],
            send_sem=s4.at[1 + k],
            recv_sem=r4.at[1 + held_chunk],
            device_id=giver(k)[0],
            device_id_type=MESH,
        )

    def take_back(m):
        return pltpu.make_async_remote_copy(
            src_ref=fin.at[piece_rows(0)],
            dst_ref=fin_in.at[piece_rows(m)],
            send_sem=s4.at[1],
            recv_sem=r4.at[1 + m],
            device_id=target(m)[0],
            device_id_type=MESH,
        )

    @pl.when(crosses)
    def _():
        swap_back.start()

    @pl.when(jnp.logical_not(crosses))
    def _():
        fin_in[0 : n.cols] = fin[0 : n.cols]

    for k in range(n.quad):
        is_me = giver(k)[1]

        @pl.when(jnp.logical_not(is_me))
        def _():
            give_back(k).start()

        @pl.when(is_me)
        def _():
            fin_in[piece_rows(held_chunk)] = fin[piece_rows(k)]

    @pl.when(crosses)
    def _():
        swap_back.wait_recv()

    for m in range(n.chunks):

        @pl.when(jnp.logical_not(target(m)[1]))
        def _():
            take_back(m).wait_recv()

    for m in range(n.chunks):
        at = n.cols + m * n.chunk_pad
        c_pad[m * n.chunk : m * n.chunk + n.chunk_pad] = fin_in[at : at + n.chunk_pad]
    c_pad[0 : n.cols] = c_pad[0 : n.cols] + fin_in[0 : n.cols]
    out[...] = c_pad[...].T[0 : n.rows, 0 : n.cols]

    @pl.when(crosses)
    def _():
        swap.wait_send()
        swap_back.wait_send()

    for m in range(n.chunks):

        @pl.when(jnp.logical_not(target(m)[1]))
        def _():
            give(m).wait_send()

    for k in range(n.quad):

        @pl.when(jnp.logical_not(giver(k)[1]))
        def _():
            give_back(k).wait_send()

    def drain(d, carry):
        share(d, me).wait_send()
        pass_on(d, peer(d), me).wait_send()
        return carry

    lax.fori_loop(1, n.plane, drain, 0)


def per_device(mesh, coefficients, integrals, targets, orbital_pairs, phases):
    rows, cols = coefficients.shape
    n = plan_of(
        mesh, (rows * mesh.shape["tile"], cols * mesh.shape["wide"]), targets.shape, integrals.shape[0]
    )
    bf16, f32 = jnp.bfloat16, jnp.float32
    slot = (n.cols + n.quad * n.chunk_pad, LANES)
    total = n.own * LANES
    dma = pltpu.SemaphoreType.DMA
    vmem, anywhere = pl.BlockSpec(memory_space=pltpu.VMEM), pl.BlockSpec(memory_space=pl.ANY)
    return pl.pallas_call(
        functools.partial(kernel, n),
        out_shape=jax.ShapeDtypeStruct((n.rows, n.cols), f32),
        in_specs=[vmem, vmem, anywhere, anywhere, anywhere],
        out_specs=vmem,
        scratch_shapes=[
            pltpu.VMEM((3, n.exc, 2 * LANES), jnp.int32),
            pltpu.VMEM((3, LANES, 2 * LANES), jnp.int32),
            pltpu.VMEM((n.pair_pad, n.pair_pad), bf16),
            pltpu.VMEM((LANES, LANES), f32),
            pltpu.VMEM(slot, bf16),
            pltpu.VMEM(slot, bf16),
            pltpu.VMEM((n.plane, *slot), bf16),
            pltpu.VMEM((n.strings, LANES), f32),
            pltpu.VMEM((2 * LANES, n.strings), bf16),
            pltpu.VMEM((total, n.strings), bf16),
            pltpu.VMEM((n.own, LANES, LANES), bf16),
            pltpu.VMEM((2 * LANES, total), bf16),
            pltpu.VMEM((2 * LANES, n.strings), f32),
            pltpu.VMEM((n.plane, *slot), bf16),
            pltpu.VMEM((n.plane, *slot), bf16),
            pltpu.VMEM(slot, f32),
            pltpu.VMEM(slot, f32),
            dma((3,)),
            dma((1 + n.chunks,)),
            dma((1 + n.quad,)),
            dma((n.plane,)),
            dma((n.plane,)),
            dma((n.plane,)),
            dma((n.plane,)),
            dma((1 + n.quad,)),
            dma((1 + n.chunks,)),
        ],
        compiler_params=pltpu.CompilerParams(
            collective_id=0, has_side_effects=True, vmem_limit_bytes=56 * 1024 * 1024
        ),
        name="sigma",
    )(coefficients, integrals, targets, orbital_pairs, phases)


def solution(mesh):
    in_specs = (P("tile", "wide"), P(), P(), P(), P())
    return jax.shard_map(
        functools.partial(per_device, mesh),
        mesh=mesh,
        in_specs=in_specs,
        out_specs=P("tile", "wide"),
        check_vma=False,
    )
```

```python
import functools
import types

import jax
import jax.numpy as jnp
from jax import lax
from jax.experimental import pallas as pl
from jax.experimental.pallas import tpu as pltpu
from jax.sharding import PartitionSpec as P

LANES = 128
MESH = pl.DeviceIdType.MESH


def plan_of(mesh, coef_shape, exc_shape, pair_count):
    tiles, wides = mesh.shape["tile"], mesh.shape["wide"]
    xs = 4 if wides == 32 else 2
    ys = wides // (2 * xs)
    strings = coef_shape[0]
    rows, cols = strings // tiles, strings // wides
    spots = xs * ys
    halves = 2 if ys % 2 == 0 else 1
    chunks = tiles // 4
    chunk = cols // chunks
    return types.SimpleNamespace(
        tiles=tiles,
        wides=wides,
        xs=xs,
        ys=ys,
        plane=2 * spots,
        spots=spots,
        halves=halves,
        width=strings // halves,
        slot=cols + (tiles // 4) * (-(-chunk // 16) * 16),
        strings=strings,
        rows=rows,
        cols=cols,
        quad=tiles // 4,
        chunks=chunks,
        chunk=chunk,
        chunk_pad=-(-chunk // 16) * 16,
        sets=xs * ys // 2,
        own=strings // (xs * ys * 2),
        exc=exc_shape[0],
        pairs=pair_count,
        pair_pad=-(-pair_count // LANES) * LANES,
        step=8,
    )


def kernel(n, coef, integ, tgt, prs, phs, out, raw, tabs, g_pad, p_part, c_pad, first, hold, gath, xt, x_all,
           t_all, w_all, u_all, part, xa, sb, rb, sa, ra, ob, oa, in_b, in_a, fin, fin_in,
           s_tab, s1, r1, s2, r2, s5, r5, s6, r6, s3b, r3b, s3a, r3a, s4, r4):
    bf16, f32 = jnp.bfloat16, jnp.float32
    tile, wide = lax.axis_index("tile"), lax.axis_index("wide")
    core, zl = lax.rem(tile, 2), tile // 2
    x, zh, y = lax.rem(wide, n.xs), lax.rem(wide // n.xs, 2), wide // (2 * n.xs)
    spot = y * n.xs + x
    x_low, zl_odd = lax.rem(x, 2), lax.rem(zl, 2)

    def device(xx, yy, zzh, zzl, cc):
        return (zzl * 2 + cc, (yy * 2 + zzh) * n.xs + xx)

    def at_spot(j):
        return device(lax.rem(j, n.xs), j // n.xs, zh, zl, core)

    def other(d):
        return lax.rem(spot + d, n.spots)

    def flip(a, b):
        return lax.rem(a + b, 2)

    partner = device(x, y, zh, zl, 1 - core)
    crosses = zh != core
    far = device(x, y, 1 - zh, zl, 1 - core)
    my_quad, my_slot = tile // n.quad, lax.rem(tile, n.quad)
    to_x = (x // 2) * 2 + flip(x_low, my_quad // 2)
    to_core = lax.rem(my_quad, 2)

    def target(m):
        zz = 2 * m + x_low
        is_me = (to_x == x) & (to_core == core) & (zz == zl)
        return device(to_x, y, zh, zz, to_core), is_me

    from_x = (x // 2) * 2 + zl_odd
    held_quad = 2 * flip(x_low, zl_odd) + core
    held_set = y * (n.xs // 2) + x // 2

    def giver(k):
        t = held_quad * n.quad + k
        is_me = (from_x == x) & (t == tile)
        return device(from_x, y, zh, t // 2, lax.rem(t, 2)), is_me

    held_chunk = zl // 2

    barrier = pltpu.get_barrier_semaphore()

    def greet_one(whom):
        pl.semaphore_signal(barrier, inc=1, device_id=whom, device_id_type=MESH)

    def greet(d, carry):
        greet_one(at_spot(other(d)))
        return carry

    @pl.when(crosses)
    def _():
        greet_one(far)

    for m in range(n.chunks):
        where_to, is_me = target(m)

        @pl.when(jnp.logical_not(is_me))
        def _():
            greet_one(where_to)

    for k in range(n.quad):
        whose, is_me = giver(k)

        @pl.when(jnp.logical_not(is_me))
        def _():
            greet_one(whose)

    greet_one(partner)
    lax.fori_loop(1, n.spots, greet, 0)

    start = (spot * 2 + core) * n.own
    window = jnp.minimum(start // LANES * LANES, n.strings - 2 * LANES)
    window = pl.multiple_of(window, LANES)
    loads = [
        pltpu.make_async_copy(ref.at[:, pl.ds(window, 2 * LANES)], raw.at[i], s_tab.at[i])
        for i, ref in enumerate((tgt, prs, phs))
    ]
    for load in loads:
        load.start()

    c_pad[...] = jnp.zeros_like(c_pad)
    c_pad[0 : n.cols, 0 : n.rows] = coef[...].astype(f32)
    first[0 : n.cols] = c_pad[0 : n.cols].astype(bf16)
    for m in range(n.chunks):
        piece = c_pad[m * n.chunk : m * n.chunk + n.chunk_pad]
        at = n.cols + m * n.chunk_pad
        first[at : at + n.chunk_pad] = piece.astype(bf16)

    g_pad[...] = jnp.zeros_like(g_pad)
    g_pad[0 : n.pairs, 0 : n.pairs] = integ[...]
    tabs[...] = jnp.zeros_like(tabs)
    for load in loads:
        load.wait()
    tabs[:, 0 : n.exc] = raw[...]

    offset = start - window
    lane = lax.broadcasted_iota(jnp.int32, (LANES, LANES), 1).astype(f32).astype(bf16)
    one, zero = jnp.ones((), bf16), jnp.zeros((), bf16)

    def spread_col(col):
        return jnp.broadcast_to(col, (LANES, LANES)).astype(bf16)

    def build(it, carry):
        shift = lax.rem(2 * 2 * LANES - offset - it * n.step, 2 * LANES)
        t = pltpu.roll(tabs[0], shift, 1)[:, 0:LANES]
        q = pltpu.roll(tabs[1], shift, 1)[:, 0:LANES]
        s = pltpu.roll(tabs[2], shift, 1)[:, 0:LANES].astype(f32)
        t_hi, t_lo = (t // LANES).astype(f32), lax.rem(t, LANES).astype(f32)
        q_hi, q_lo = (q // LANES).astype(f32), lax.rem(q, LANES).astype(f32)
        for u in range(n.step):
            hi, lo = spread_col(q_hi[:, u : u + 1]), spread_col(q_lo[:, u : u + 1])
            sign = spread_col(s[:, u : u + 1])
            hot = jnp.where(lo == lane, sign, zero)
            for kt in range(n.pair_pad // LANES):
                p_part[u * LANES : (u + 1) * LANES, kt * LANES : (kt + 1) * LANES] = jnp.where(
                    hi == kt, hot, zero
                )
        picked = lax.dot_general(
            p_part[...], g_pad[...], (((1,), (1,)), ((), ())), preferred_element_type=f32
        ).astype(bf16)
        for u in range(n.step):
            b = it * n.step + u
            rows = pl.ds(pl.multiple_of(b * LANES, LANES), LANES)
            hi, lo = spread_col(t_hi[:, u : u + 1]), spread_col(t_lo[:, u : u + 1])
            hot = jnp.where(lo == lane, one, zero)
            for kt in range(n.strings // LANES):
                t_all[rows, kt * LANES : (kt + 1) * LANES] = jnp.where(hi == kt, hot, zero)
        for u in range(n.step):
            rows = slice(u * LANES, (u + 1) * LANES)
            w_all[it * n.step + u] = lax.dot_general(
                picked[rows], p_part[rows], (((1,), (1,)), ((), ())), preferred_element_type=f32
            ).astype(bf16)
        return carry

    builds = n.own // n.step
    cut_a, cut_b = max(1, builds // 6), max(1, builds * 2 // 3)
    lax.fori_loop(0, cut_a, build, 0)

    itself = jnp.int32(0)
    for m in range(n.chunks):
        itself = itself + target(m)[1].astype(jnp.int32)
    expected = n.spots + n.chunks + n.quad - 2 * itself + crosses.astype(jnp.int32)
    pl.semaphore_wait(barrier, expected)

    def piece_rows(k):
        return pl.ds(pl.multiple_of(n.cols + k * n.chunk_pad, 16), n.chunk_pad)

    swap = pltpu.make_async_remote_copy(
        src_ref=first.at[pl.ds(0, n.cols)],
        dst_ref=hold.at[pl.ds(0, n.cols)],
        send_sem=s1.at[0],
        recv_sem=r1.at[0],
        device_id=far,
        device_id_type=MESH,
    )

    def give(m):
        return pltpu.make_async_remote_copy(
            src_ref=first.at[piece_rows(m)],
            dst_ref=hold.at[piece_rows(my_slot)],
            send_sem=s1.at[1 + m],
            recv_sem=r1.at[1 + my_slot],
            device_id=target(m)[0],
            device_id_type=MESH,
        )

    def take(k):
        return pltpu.make_async_remote_copy(
            src_ref=first.at[piece_rows(0)],
            dst_ref=hold.at[piece_rows(k)],
            send_sem=s1.at[1],
            recv_sem=r1.at[1 + k],
            device_id=giver(k)[0],
            device_id_type=MESH,
        )

    @pl.when(crosses)
    def _():
        swap.start()

    @pl.when(jnp.logical_not(crosses))
    def _():
        hold[0 : n.cols] = first[0 : n.cols]

    for m in range(n.chunks):
        is_me = target(m)[1]

        @pl.when(jnp.logical_not(is_me))
        def _():
            give(m).start()

        @pl.when(is_me)
        def _():
            hold[piece_rows(my_slot)] = first[piece_rows(m)]

    lax.fori_loop(cut_a, cut_b, build, 0)

    @pl.when(crosses)
    def _():
        swap.wait_recv()

    for k in range(n.quad):

        @pl.when(jnp.logical_not(giver(k)[1]))
        def _():
            take(k).wait_recv()

    def share(to, frm):
        return pltpu.make_async_remote_copy(
            src_ref=hold,
            dst_ref=gath.at[core, frm],
            send_sem=s2.at[to],
            recv_sem=r2.at[frm],
            device_id=at_spot(to),
            device_id_type=MESH,
        )

    def relay(j, side):
        return pltpu.make_async_remote_copy(
            src_ref=gath.at[side, j],
            dst_ref=gath.at[side, j],
            send_sem=s5.at[j],
            recv_sem=r5.at[j],
            device_id=partner,
            device_id_type=MESH,
        )

    def start_share(d, carry):
        share(other(d), spot).start()
        return carry

    lax.fori_loop(1, n.spots, start_share, 0)
    gath[core, spot] = hold[...]
    relay(spot, core).start()

    lax.fori_loop(cut_b, builds, build, 0)

    def hand_on(d, carry):
        share(spot, other(d)).wait_recv()
        relay(other(d), core).start()
        return carry

    lax.fori_loop(1, n.spots, hand_on, 0)

    def wait_relay(j, carry):
        relay(j, 1 - core).wait_recv()
        return carry

    lax.fori_loop(0, n.spots, wait_relay, 0)

    for w in range(n.plane):
        yy, cc, xx = w // (2 * n.xs), w // n.xs % 2, w % n.xs
        xt[w * n.cols : (w + 1) * n.cols] = gath[cc, yy * n.xs + xx, 0 : n.cols].astype(f32)
    for kt in range(n.strings // LANES):
        at = slice(kt * LANES, (kt + 1) * LANES)
        x_all[0:LANES, at] = xt[at].T.astype(bf16)

    lane_i = lax.broadcasted_iota(jnp.int32, (LANES, LANES), 1)

    def alpha_piece(t):
        quad, slot = t // n.quad, t % n.quad
        at = n.cols + slot * n.chunk_pad
        pieces = []
        for s in range(n.sets):
            yy, xh = s // (n.xs // 2), s % (n.xs // 2)
            xx = 2 * xh + flip(zl_odd, quad // 2)
            pieces.append(gath[quad % 2, yy * n.xs + xx, at : at + n.chunk_pad].astype(f32))
        short = LANES - n.sets * n.chunk_pad
        if short:
            pieces.append(jnp.zeros((short, LANES), f32))
        return jnp.concatenate(pieces, axis=0)

    for four in range(n.tiles // 4):
        p0, p1, p2, p3 = (alpha_piece(4 * four + i) for i in range(4))
        p1, p2, p3 = pltpu.roll(p1, 96, 1), pltpu.roll(p2, 64, 1), pltpu.roll(p3, 32, 1)
        tiles3 = (
            jnp.where(lane_i < 96, p0, p1),
            jnp.where(lane_i < 64, p1, p2),
            jnp.where(lane_i < 32, p2, p3),
        )
        for i, value in enumerate(tiles3):
            at = (3 * four + i) * LANES
            x_all[LANES : 2 * LANES, at : at + LANES] = value.astype(bf16)

    many = min(8, n.own)

    def couple(it, carry):
        rows = pl.ds(pl.multiple_of(it * many * LANES, many * LANES), many * LANES)
        v = lax.dot_general(
            x_all[...], t_all[rows, :], (((1,), (1,)), ((), ())), preferred_element_type=f32
        ).astype(bf16)
        for u in range(many):
            value = jnp.dot(
                v[:, u * LANES : (u + 1) * LANES], w_all[it * many + u], preferred_element_type=f32
            )
            at = pl.ds(pl.multiple_of((it * many + u) * LANES, LANES), LANES)
            u_all[:, at] = value.astype(bf16)
        return carry

    lax.fori_loop(0, n.own // many, couple, 0)

    block = n.xs * n.cols

    def block_rows(yy, cc):
        return pl.ds(pl.multiple_of((yy * 2 + cc) * block, 16), block)

    def ys_of(h):
        return range(h * n.ys // n.halves, (h + 1) * n.ys // n.halves)

    def bases_of(h):
        return range(h * 4 // n.halves, (h + 1) * 4 // n.halves, 2)

    def cross_b(yy, cc):
        return pltpu.make_async_remote_copy(
            src_ref=sb.at[block_rows(yy, cc)],
            dst_ref=rb.at[block_rows(yy, cc)],
            send_sem=s6.at[yy],
            recv_sem=r6.at[yy],
            device_id=partner,
            device_id_type=MESH,
        )

    def cross_a(base, cc):
        return pltpu.make_async_remote_copy(
            src_ref=sa.at[base + cc],
            dst_ref=ra.at[base + cc],
            send_sem=s6.at[n.ys + base // 2],
            recv_sem=r6.at[n.ys + base // 2],
            device_id=partner,
            device_id_type=MESH,
        )

    def scatter(h):
        at = slice(h * n.width, (h + 1) * n.width)
        part[:, at] = jnp.dot(u_all[...], t_all[:, at], preferred_element_type=f32)

    def exchange(h):
        first_tile = h * n.width // LANES
        for kt in range(first_tile, first_tile + n.width // LANES):
            at = slice(kt * LANES, (kt + 1) * LANES)
            xt[at] = part[0:LANES, at].T
        for yy in ys_of(h):
            rows = block_rows(yy, 1 - core)
            sb[rows] = xt[rows].astype(bf16)
            cross_b(yy, 1 - core).start()
        per = n.tiles // 4 // n.halves
        for four in range(h * per, (h + 1) * per):
            t0, t1, t2 = (
                part[LANES : 2 * LANES, (3 * four + i) * LANES : (3 * four + i + 1) * LANES]
                for i in range(3)
            )
            roll = functools.partial(pltpu.roll, axis=1)
            values = (
                t0,
                jnp.where(lane_i < 32, roll(t0, 32), roll(t1, 32)),
                jnp.where(lane_i < 64, roll(t1, 64), roll(t2, 64)),
                roll(t2, 96),
            )
            for i, value in enumerate(values):
                t = 4 * four + i
                quad, slot = t // n.quad, t % n.quad
                for s in range(n.sets):
                    xa[quad, s, slot * n.chunk_pad : (slot + 1) * n.chunk_pad] = value[
                        s * n.chunk_pad : (s + 1) * n.chunk_pad
                    ]
        for base in bases_of(h):
            sa[base + 1 - core] = xa[base + 1 - core].astype(bf16)
            cross_a(base, 1 - core).start()

    def send_b(yy, xx):
        rows = pl.ds(pl.multiple_of(((yy * 2 + core) * n.xs + xx) * n.cols, 16), n.cols)
        to = yy * n.xs + xx
        return pltpu.make_async_remote_copy(
            src_ref=ob.at[rows],
            dst_ref=in_b.at[spot],
            send_sem=s3b.at[to],
            recv_sem=r3b.at[spot],
            device_id=at_spot(to),
            device_id_type=MESH,
        )

    def send_a(base, s):
        to = (s // (n.xs // 2)) * n.xs + 2 * lax.rem(s, n.xs // 2) + flip(zl_odd, base // 2)
        copy = pltpu.make_async_remote_copy(
            src_ref=oa.at[base + core, s],
            dst_ref=in_a.at[spot],
            send_sem=s3a.at[to],
            recv_sem=r3a.at[spot],
            device_id=at_spot(to),
            device_id_type=MESH,
        )
        return copy, to

    def spread_out(h):
        for yy in ys_of(h):
            rows = block_rows(yy, core)
            cross_b(yy, core).wait_recv()
            total = xt[rows] + rb[rows].astype(f32)
            xt[rows] = total
            ob[rows] = total.astype(bf16)
            for i in range(n.xs):
                xx = lax.rem(x + i, n.xs)

                @pl.when(jnp.logical_or(xx != x, y != yy))
                def _():
                    send_b(yy, xx).start()

        for base in bases_of(h):
            cross_a(base, core).wait_recv()
            total = xa[base + core] + ra[base + core].astype(f32)
            xa[base + core] = total
            oa[base + core] = total.astype(bf16)
            for i in range(n.sets):
                copy, to = send_a(base, lax.rem(held_set + i, n.sets))

                @pl.when(to != spot)
                def _():
                    copy.start()

    scatter(0)
    exchange(0)
    for h in range(1, n.halves):
        scatter(h)
        spread_out(h - 1)
        exchange(h)
    spread_out(n.halves - 1)

    mine = pl.ds(pl.multiple_of(((y * 2 + core) * n.xs + x) * n.cols, 16), n.cols)
    fin[0 : n.cols] = xt[mine]
    fin[n.cols :] = xa[held_quad, held_set]

    def add_in(d, carry):
        j = other(d)
        pltpu.make_async_remote_copy(
            src_ref=ob.at[pl.ds(0, n.cols)],
            dst_ref=in_b.at[j],
            send_sem=s3b.at[j],
            recv_sem=r3b.at[j],
            device_id=at_spot(j),
            device_id_type=MESH,
        ).wait_recv()
        fin[0 : n.cols] += in_b[j].astype(f32)
        pltpu.make_async_remote_copy(
            src_ref=oa.at[0, 0],
            dst_ref=in_a.at[j],
            send_sem=s3a.at[j],
            recv_sem=r3a.at[j],
            device_id=at_spot(j),
            device_id_type=MESH,
        ).wait_recv()
        fin[n.cols :] += in_a[j].astype(f32)
        return carry

    lax.fori_loop(1, n.spots, add_in, 0)

    swap_back = pltpu.make_async_remote_copy(
        src_ref=fin.at[pl.ds(0, n.cols)],
        dst_ref=fin_in.at[pl.ds(0, n.cols)],
        send_sem=s4.at[0],
        recv_sem=r4.at[0],
        device_id=far,
        device_id_type=MESH,
    )

    def give_back(k):
        return pltpu.make_async_remote_copy(
            src_ref=fin.at[piece_rows(k)],
            dst_ref=fin_in.at[piece_rows(held_chunk)],
            send_sem=s4.at[1 + k],
            recv_sem=r4.at[1 + held_chunk],
            device_id=giver(k)[0],
            device_id_type=MESH,
        )

    def take_back(m):
        return pltpu.make_async_remote_copy(
            src_ref=fin.at[piece_rows(0)],
            dst_ref=fin_in.at[piece_rows(m)],
            send_sem=s4.at[1],
            recv_sem=r4.at[1 + m],
            device_id=target(m)[0],
            device_id_type=MESH,
        )

    @pl.when(crosses)
    def _():
        swap_back.start()

    @pl.when(jnp.logical_not(crosses))
    def _():
        fin_in[0 : n.cols] = fin[0 : n.cols]

    for k in range(n.quad):
        is_me = giver(k)[1]

        @pl.when(jnp.logical_not(is_me))
        def _():
            give_back(k).start()

        @pl.when(is_me)
        def _():
            fin_in[piece_rows(held_chunk)] = fin[piece_rows(k)]

    @pl.when(crosses)
    def _():
        swap.wait_send()

    for m in range(n.chunks):

        @pl.when(jnp.logical_not(target(m)[1]))
        def _():
            give(m).wait_send()

    def drain(d, carry):
        j = other(d)
        share(j, spot).wait_send()
        send_b(j // n.xs, lax.rem(j, n.xs)).wait_send()
        pltpu.make_async_remote_copy(
            src_ref=oa.at[0, 0],
            dst_ref=in_a.at[j],
            send_sem=s3a.at[j],
            recv_sem=r3a.at[j],
            device_id=at_spot(j),
            device_id_type=MESH,
        ).wait_send()
        return carry

    lax.fori_loop(1, n.spots, drain, 0)

    def drain_relay(j, carry):
        relay(j, core).wait_send()
        return carry

    lax.fori_loop(0, n.spots, drain_relay, 0)
    for yy in range(n.ys):
        cross_b(yy, 1 - core).wait_send()
    for base in (0, 2):
        cross_a(base, 1 - core).wait_send()

    @pl.when(crosses)
    def _():
        swap_back.wait_recv()
        swap_back.wait_send()

    for m in range(n.chunks):

        @pl.when(jnp.logical_not(target(m)[1]))
        def _():
            take_back(m).wait_recv()

    for k in range(n.quad):

        @pl.when(jnp.logical_not(giver(k)[1]))
        def _():
            give_back(k).wait_send()

    for m in range(n.chunks):
        at = n.cols + m * n.chunk_pad
        c_pad[m * n.chunk : m * n.chunk + n.chunk_pad] = fin_in[at : at + n.chunk_pad]
    out[...] = c_pad[0 : n.cols, 0 : n.rows] + fin_in[0 : n.cols, 0 : n.rows]


def per_device(mesh, coefficients, integrals, targets, orbital_pairs, phases):
    rows, cols = coefficients.shape
    n = plan_of(
        mesh, (rows * mesh.shape["tile"], cols * mesh.shape["wide"]), targets.shape, integrals.shape[0]
    )
    bf16, f32 = jnp.bfloat16, jnp.float32
    total = n.own * LANES
    alpha = n.slot - n.cols
    dma = pltpu.SemaphoreType.DMA
    vmem, anywhere = pl.BlockSpec(memory_space=pltpu.VMEM), pl.BlockSpec(memory_space=pl.ANY)
    sigma_t = pl.pallas_call(
        functools.partial(kernel, n),
        out_shape=jax.ShapeDtypeStruct((n.cols, n.rows), f32),
        in_specs=[vmem, vmem, anywhere, anywhere, anywhere],
        out_specs=vmem,
        scratch_shapes=[
            pltpu.VMEM((3, n.exc, 2 * LANES), jnp.int32),
            pltpu.VMEM((3, LANES, 2 * LANES), jnp.int32),
            pltpu.VMEM((n.pair_pad, n.pair_pad), bf16),
            pltpu.VMEM((n.step * LANES, n.pair_pad), bf16),
            pltpu.VMEM((LANES, LANES), f32),
            pltpu.VMEM((n.slot, LANES), bf16),
            pltpu.VMEM((n.slot, LANES), bf16),
            pltpu.VMEM((2, n.spots, n.slot, LANES), bf16),
            pltpu.VMEM((n.strings, LANES), f32),
            pltpu.VMEM((2 * LANES, n.strings), bf16),
            pltpu.VMEM((total, n.strings), bf16),
            pltpu.VMEM((n.own, LANES, LANES), bf16),
            pltpu.VMEM((2 * LANES, total), bf16),
            pltpu.VMEM((2 * LANES, n.strings), f32),
            pltpu.VMEM((4, n.sets, alpha, LANES), f32),
            pltpu.VMEM((n.strings, LANES), bf16),
            pltpu.VMEM((n.strings, LANES), bf16),
            pltpu.VMEM((4, n.sets, alpha, LANES), bf16),
            pltpu.VMEM((4, n.sets, alpha, LANES), bf16),
            pltpu.VMEM((n.strings, LANES), bf16),
            pltpu.VMEM((4, n.sets, alpha, LANES), bf16),
            pltpu.VMEM((n.spots, n.cols, LANES), bf16),
            pltpu.VMEM((n.spots, alpha, LANES), bf16),
            pltpu.VMEM((n.slot, LANES), f32),
            pltpu.VMEM((n.slot, LANES), f32),
            dma((3,)),
            dma((1 + n.chunks,)),
            dma((1 + n.quad,)),
            dma((n.spots,)),
            dma((n.spots,)),
            dma((n.spots,)),
            dma((n.spots,)),
            dma((n.ys + 2,)),
            dma((n.ys + 2,)),
            dma((n.spots,)),
            dma((n.spots,)),
            dma((n.spots,)),
            dma((n.spots,)),
            dma((1 + n.quad,)),
            dma((1 + n.chunks,)),
        ],
        compiler_params=pltpu.CompilerParams(
            collective_id=0, has_side_effects=True, vmem_limit_bytes=56 * 1024 * 1024
        ),
        name="sigma",
    )(coefficients.T, integrals, targets, orbital_pairs, phases)
    return sigma_t.T


def solution(mesh):
    in_specs = (P("tile", "wide"), P(), P(), P(), P())
    return jax.shard_map(
        functools.partial(per_device, mesh),
        mesh=mesh,
        in_specs=in_specs,
        out_specs=P("tile", "wide"),
        check_vma=False,
    )
```

```python
import functools
import types

import jax
import jax.numpy as jnp
from jax import lax
from jax.experimental import pallas as pl
from jax.experimental.pallas import tpu as pltpu
from jax.sharding import PartitionSpec as P

LANES = 128
MESH = pl.DeviceIdType.MESH


def plan_of(mesh, coef_shape, exc_shape, pair_count):
    tiles, wides = mesh.shape["tile"], mesh.shape["wide"]
    xs = 4 if wides == 32 else 2
    ys = wides // (2 * xs)
    zs = tiles // 2
    strings = coef_shape[0]
    ranges = strings // (3 * LANES)
    return types.SimpleNamespace(
        tiles=tiles,
        xs=xs,
        ys=ys,
        zs=zs,
        spots=xs * ys,
        strings=strings,
        rows=strings // tiles,
        cols=strings // wides,
        own=strings // (xs * ys * 2),
        exc=exc_shape[0],
        pairs=pair_count,
        pair_pad=-(-pair_count // LANES) * LANES,
        step=8,
        ranges=ranges,
        order=sorted(range(ranges), key=lambda h: -abs(2 * h - ranges + 1)),
        width=strings // ranges,
    )


def kernel(n, coef, integ, tgt, prs, phs, out, raw, tabs, g_pad, p_part, c_pad, first, hold, gath_b, gath_a,
           xt, x_all, t_all, w_all, u_all, part, xa, sb, rb, ob, sa, ra, sx, rx, oa, in_b, in_a, fin, fin_in,
           s_tab, s1, r1, s2b, r2b, s5b, r5b, s2a, r2a, sxa, rxa, s5a, r5a, s6b, r6b, s6a, r6a,
           s3b, r3b, s7, r7, s8, r8, s4, r4):
    bf16, f32 = jnp.bfloat16, jnp.float32
    tile, wide = lax.axis_index("tile"), lax.axis_index("wide")
    core, zl = lax.rem(tile, 2), tile // 2
    x, zh, y = lax.rem(wide, n.xs), lax.rem(wide // n.xs, 2), wide // (2 * n.xs)
    spot = y * n.xs + x
    x_low, x_high = lax.rem(x, 2), x // 2

    def device(xx, yy, zzh, zzl, cc):
        return (zzl * 2 + cc, (yy * 2 + zzh) * n.xs + xx)

    def at_spot(j):
        return device(lax.rem(j, n.xs), j // n.xs, zh, zl, core)

    def on_line(z):
        return device(x, y, zh, z, core)

    def other(d):
        return lax.rem(spot + d, n.spots)

    def other_z(d):
        return lax.rem(zl + d, n.zs)

    partner = device(x, y, zh, zl, 1 - core)
    mate = device(x_high * 2 + 1 - x_low, y, zh, zl, core)
    half = n.zs // 2
    far_z = lax.rem(zl + half + n.zs * core, 2 * n.zs)
    far_out = device(x, y, far_z // n.zs, lax.rem(far_z, n.zs), zh)
    back_z = zh * n.zs + zl + 2 * n.zs - half
    back_zl = lax.rem(back_z, n.zs)
    far_in = device(x, y, core, back_zl, lax.rem(back_z - back_zl, 2 * n.zs) // n.zs)

    def remote(src, dst, send, recv, to):
        return pltpu.make_async_remote_copy(
            src_ref=src, dst_ref=dst, send_sem=send, recv_sem=recv, device_id=to, device_id_type=MESH
        )

    place = lax.rem(y * (n.xs // 2) + x_high + zl, n.zs)
    start = ((x_low * 2 + core) * n.zs + place) * n.own
    window = jnp.minimum(start // LANES * LANES, n.strings - 2 * LANES)
    window = pl.multiple_of(window, LANES)
    loads = [
        pltpu.make_async_copy(ref.at[:, pl.ds(window, 2 * LANES)], raw.at[i], s_tab.at[i])
        for i, ref in enumerate((tgt, prs, phs))
    ]
    for load in loads:
        load.start()

    barrier = pltpu.get_barrier_semaphore()

    def greet(whom):
        pl.semaphore_signal(barrier, inc=1, device_id=whom, device_id_type=MESH)

    def greet_line(d, carry):
        greet(on_line(other_z(d)))
        return carry

    def greet_plane(d, carry):
        greet(at_spot(other(d)))
        return carry

    greet(far_out)
    greet(far_in)
    lax.fori_loop(1, n.zs, greet_line, 0)
    lax.fori_loop(1, n.spots, greet_plane, 0)
    greet(partner)

    c_pad[...] = jnp.zeros_like(c_pad)
    c_pad[:, 0 : n.rows] = coef[...].astype(f32)
    first[...] = c_pad[...].astype(bf16)

    g_pad[...] = jnp.zeros_like(g_pad)
    g_pad[0 : n.pairs, 0 : n.pairs] = integ[...]
    tabs[...] = jnp.zeros_like(tabs)
    for load in loads:
        load.wait()
    tabs[:, 0 : n.exc] = raw[...]

    offset = start - window
    lane = lax.broadcasted_iota(jnp.int32, (LANES, LANES), 1).astype(f32).astype(bf16)
    one, zero = jnp.ones((), bf16), jnp.zeros((), bf16)

    def spread_col(col):
        return jnp.broadcast_to(col, (LANES, LANES)).astype(bf16)

    def build(it, carry):
        shift = lax.rem(2 * 2 * LANES - offset - it * n.step, 2 * LANES)
        t = pltpu.roll(tabs[0], shift, 1)[:, 0:LANES]
        q = pltpu.roll(tabs[1], shift, 1)[:, 0:LANES]
        s = pltpu.roll(tabs[2], shift, 1)[:, 0:LANES].astype(f32)
        t_hi, t_lo = (t // LANES).astype(f32), lax.rem(t, LANES).astype(f32)
        q_hi, q_lo = (q // LANES).astype(f32), lax.rem(q, LANES).astype(f32)
        for u in range(n.step):
            hi, lo = spread_col(q_hi[:, u : u + 1]), spread_col(q_lo[:, u : u + 1])
            sign = spread_col(s[:, u : u + 1])
            hot = jnp.where(lo == lane, sign, zero)
            for kt in range(n.pair_pad // LANES):
                p_part[u * LANES : (u + 1) * LANES, kt * LANES : (kt + 1) * LANES] = jnp.where(
                    hi == kt, hot, zero
                )
        picked = lax.dot_general(
            p_part[...], g_pad[...], (((1,), (1,)), ((), ())), preferred_element_type=f32
        ).astype(bf16)
        for u in range(n.step):
            b = it * n.step + u
            rows = pl.ds(pl.multiple_of(b * LANES, LANES), LANES)
            hi, lo = spread_col(t_hi[:, u : u + 1]), spread_col(t_lo[:, u : u + 1])
            hot = jnp.where(lo == lane, one, zero)
            for kt in range(n.strings // LANES):
                t_all[rows, kt * LANES : (kt + 1) * LANES] = jnp.where(hi == kt, hot, zero)
        for u in range(n.step):
            rows = slice(u * LANES, (u + 1) * LANES)
            w_all[it * n.step + u] = lax.dot_general(
                picked[rows], p_part[rows], (((1,), (1,)), ((), ())), preferred_element_type=f32
            ).astype(bf16)
        return carry

    builds = n.own // n.step
    cut_a, cut_b = max(1, builds // 3), max(1, builds * 5 // 6)
    lax.fori_loop(0, cut_a, build, 0)

    pl.semaphore_wait(barrier, 2 + n.zs - 1 + n.spots - 1 + 1)

    def line(to, frm):
        return remote(first, gath_a.at[core, x_low, frm], s2a.at[to], r2a.at[frm], on_line(to))

    def to_mate(z, side):
        ref = gath_a.at[core, side, z]
        return remote(ref, ref, sxa.at[z], rxa.at[z], mate)

    def relay_a(z, side, cc):
        ref = gath_a.at[cc, side, z]
        return remote(ref, ref, s5a.at[side, z], r5a.at[side, z], partner)

    def share(to, frm):
        return remote(hold, gath_b.at[core, frm], s2b.at[to], r2b.at[frm], at_spot(to))

    def relay_b(j, cc):
        ref = gath_b.at[cc, j]
        return remote(ref, ref, s5b.at[j], r5b.at[j], partner)

    forth = remote(first, hold, s1.at[0], r1.at[0], far_out)
    forth.start()

    def start_line(d, carry):
        line(other_z(d), zl).start()
        return carry

    lax.fori_loop(1, n.zs, start_line, 0)
    gath_a[core, x_low, zl] = first[...]
    to_mate(zl, x_low).start()
    relay_a(zl, x_low, core).start()

    lax.fori_loop(cut_a, cut_b, build, 0)

    forth.wait_recv()

    def start_share(d, carry):
        share(other(d), spot).start()
        return carry

    lax.fori_loop(1, n.spots, start_share, 0)
    gath_b[core, spot] = hold[...]
    relay_b(spot, core).start()

    lax.fori_loop(cut_b, builds, build, 0)

    def hand_line(d, carry):
        z = other_z(d)
        line(zl, z).wait_recv()
        to_mate(z, x_low).start()
        relay_a(z, x_low, core).start()
        return carry

    lax.fori_loop(1, n.zs, hand_line, 0)

    def hand_plane(d, carry):
        j = other(d)
        share(spot, j).wait_recv()
        relay_b(j, core).start()
        return carry

    lax.fori_loop(1, n.spots, hand_plane, 0)

    def hand_mate(d, carry):
        z = other_z(d)
        to_mate(z, 1 - x_low).wait_recv()
        relay_a(z, 1 - x_low, core).start()
        return carry

    lax.fori_loop(0, n.zs, hand_mate, 0)

    def wait_relay_b(j, carry):
        relay_b(j, 1 - core).wait_recv()
        return carry

    lax.fori_loop(0, n.spots, wait_relay_b, 0)

    for w in range(2 * n.spots):
        yy, cc, xx = w // (2 * n.xs), w // n.xs % 2, w % n.xs
        xt[w * n.cols : (w + 1) * n.cols] = gath_b[cc, yy * n.xs + xx].astype(f32)
    for kt in range(n.strings // LANES):
        at = slice(kt * LANES, (kt + 1) * LANES)
        x_all[0:LANES, at] = xt[at].T.astype(bf16)

    def wait_relay_a(z, carry):
        relay_a(z, 0, 1 - core).wait_recv()
        relay_a(z, 1, 1 - core).wait_recv()
        return carry

    lax.fori_loop(0, n.zs, wait_relay_a, 0)

    lane_i = lax.broadcasted_iota(jnp.int32, (LANES, LANES), 1)
    spare = jnp.zeros((LANES - 2 * n.cols, LANES), f32)

    def alpha_piece(t):
        low, high = (gath_a[t % 2, side, t // 2].astype(f32) for side in range(2))
        return jnp.concatenate([low, high, spare], axis=0)

    for four in range(n.tiles // 4):
        p0, p1, p2, p3 = (alpha_piece(4 * four + i) for i in range(4))
        p1, p2, p3 = pltpu.roll(p1, 96, 1), pltpu.roll(p2, 64, 1), pltpu.roll(p3, 32, 1)
        tiles3 = (
            jnp.where(lane_i < 96, p0, p1),
            jnp.where(lane_i < 64, p1, p2),
            jnp.where(lane_i < 32, p2, p3),
        )
        for i, value in enumerate(tiles3):
            at = (3 * four + i) * LANES
            x_all[LANES : 2 * LANES, at : at + LANES] = value.astype(bf16)

    many = min(8, n.own)

    def couple(it, carry):
        rows = pl.ds(pl.multiple_of(it * many * LANES, many * LANES), many * LANES)
        v = lax.dot_general(
            x_all[...], t_all[rows, :], (((1,), (1,)), ((), ())), preferred_element_type=f32
        ).astype(bf16)
        for u in range(many):
            value = jnp.dot(
                v[:, u * LANES : (u + 1) * LANES], w_all[it * many + u], preferred_element_type=f32
            )
            at = pl.ds(pl.multiple_of((it * many + u) * LANES, LANES), LANES)
            u_all[:, at] = value.astype(bf16)
        return carry

    lax.fori_loop(0, n.own // many, couple, 0)

    block = n.xs * n.cols
    keep = pl.ds(pl.multiple_of(x_low * n.cols, 16), n.cols)
    pass_on = pl.ds(pl.multiple_of((1 - x_low) * n.cols, 16), n.cols)

    def block_rows(yy, cc):
        return pl.ds(pl.multiple_of((yy * 2 + cc) * block, 16), block)

    def ys_of(h):
        return range(h * n.ys // n.ranges, (h + 1) * n.ys // n.ranges)

    def zs_of(h):
        return range(h * n.zs // n.ranges, (h + 1) * n.zs // n.ranges)

    def cross_b(yy, cc):
        rows = block_rows(yy, cc)
        return remote(sb.at[rows], rb.at[rows], s6b.at[yy], r6b.at[yy], partner)

    def cross_a(z, cc):
        return remote(sa.at[2 * z + cc], ra.at[2 * z + cc], s6a.at[z], r6a.at[z], partner)

    def across(z):
        return remote(sx.at[z], rx.at[z], s7.at[z], r7.at[z], mate)

    def down_line(to, frm):
        return remote(oa.at[to], in_a.at[frm], s8.at[to], r8.at[frm], on_line(to))

    def to_plane(rows, to, frm):
        return remote(ob.at[rows], in_b.at[frm], s3b.at[to], r3b.at[frm], at_spot(to))

    def scatter(h):
        at = slice(h * n.width, (h + 1) * n.width)
        part[:, at] = jnp.dot(u_all[...], t_all[:, at], preferred_element_type=f32)

    def sum_cores(h):
        t0, t1, t2 = (
            part[LANES : 2 * LANES, (3 * h + i) * LANES : (3 * h + i + 1) * LANES] for i in range(3)
        )
        roll = functools.partial(pltpu.roll, axis=1)
        values = (
            t0,
            jnp.where(lane_i < 32, roll(t0, 32), roll(t1, 32)),
            jnp.where(lane_i < 64, roll(t1, 64), roll(t2, 64)),
            roll(t2, 96),
        )
        for i, value in enumerate(values):
            xa[4 * h + i] = value[0 : 2 * n.cols]
        for z in zs_of(h):
            sa[2 * z + 1 - core] = xa[2 * z + 1 - core].astype(bf16)
            cross_a(z, 1 - core).start()
        for kt in range(3 * h, 3 * h + 3):
            at = slice(kt * LANES, (kt + 1) * LANES)
            xt[at] = part[0:LANES, at].T
        for yy in ys_of(h):
            rows = block_rows(yy, 1 - core)
            sb[rows] = xt[rows].astype(bf16)
            cross_b(yy, 1 - core).start()

    def sum_mates(h):
        for z in zs_of(h):
            cross_a(z, core).wait_recv()
            xa[2 * z + core] = xa[2 * z + core] + ra[2 * z + core].astype(f32)
            sx[z] = xa[2 * z + core, pass_on].astype(bf16)
            across(z).start()
        for yy in ys_of(h):
            rows = block_rows(yy, core)
            cross_b(yy, core).wait_recv()
            total = xt[rows] + rb[rows].astype(f32)
            xt[rows] = total
            ob[rows] = total.astype(bf16)
            for i in range(n.xs):
                xx = lax.rem(x + i, n.xs)
                rows = pl.ds(pl.multiple_of(((yy * 2 + core) * n.xs + xx) * n.cols, 16), n.cols)

                @pl.when(jnp.logical_or(xx != x, y != yy))
                def _():
                    to_plane(rows, yy * n.xs + xx, spot).start()

    def sum_line(h):
        for z in zs_of(h):
            across(z).wait_recv()
            total = xa[2 * z + core, keep] + rx[z].astype(f32)
            xa[2 * z + core, keep] = total
            oa[z] = total.astype(bf16)

            @pl.when(z != zl)
            def _():
                down_line(z, zl).start()

    for i in range(n.ranges + 2):
        if i < n.ranges:
            scatter(n.order[i])
        if 0 <= i - 2 < n.ranges:
            sum_line(n.order[i - 2])
        if 0 <= i - 1 < n.ranges:
            sum_mates(n.order[i - 1])
        if i < n.ranges:
            sum_cores(n.order[i])

    mine = pl.ds(pl.multiple_of(((y * 2 + core) * n.xs + x) * n.cols, 16), n.cols)
    fin[...] = xt[mine]

    def add_plane(d, carry):
        j = other(d)
        to_plane(pl.ds(0, n.cols), spot, j).wait_recv()
        fin[...] += in_b[j].astype(f32)
        return carry

    lax.fori_loop(1, n.spots, add_plane, 0)
    back = remote(fin, fin_in, s4.at[0], r4.at[0], far_in)
    back.start()

    c_pad[...] = xa[2 * zl + core, keep]

    def add_line(d, carry):
        z = other_z(d)
        down_line(zl, z).wait_recv()
        c_pad[...] += in_a[z].astype(f32)
        return carry

    lax.fori_loop(1, n.zs, add_line, 0)

    forth.wait_send()

    def drain_line(d, carry):
        z = other_z(d)
        line(z, zl).wait_send()
        down_line(z, zl).wait_send()
        return carry

    lax.fori_loop(1, n.zs, drain_line, 0)

    def drain_line_all(z, carry):
        to_mate(z, x_low).wait_send()
        relay_a(z, 0, core).wait_send()
        relay_a(z, 1, core).wait_send()
        cross_a(z, 1 - core).wait_send()
        across(z).wait_send()
        return carry

    lax.fori_loop(0, n.zs, drain_line_all, 0)

    def drain_plane(d, carry):
        j = other(d)
        share(j, spot).wait_send()
        to_plane(pl.ds(0, n.cols), j, spot).wait_send()
        return carry

    lax.fori_loop(1, n.spots, drain_plane, 0)

    def drain_plane_all(j, carry):
        relay_b(j, core).wait_send()
        return carry

    lax.fori_loop(0, n.spots, drain_plane_all, 0)
    for yy in range(n.ys):
        cross_b(yy, 1 - core).wait_send()

    back.wait_recv()
    out[...] = c_pad[:, 0 : n.rows] + fin_in[:, 0 : n.rows]
    back.wait_send()


def per_device(mesh, coefficients, integrals, targets, orbital_pairs, phases):
    rows, cols = coefficients.shape
    n = plan_of(
        mesh, (rows * mesh.shape["tile"], cols * mesh.shape["wide"]), targets.shape, integrals.shape[0]
    )
    bf16, f32 = jnp.bfloat16, jnp.float32
    total = n.own * LANES
    piece = (n.cols, LANES)
    dma, vmem = pltpu.SemaphoreType.DMA, pltpu.VMEM
    here, anywhere = pl.BlockSpec(memory_space=pltpu.VMEM), pl.BlockSpec(memory_space=pl.ANY)
    sigma_t = pl.pallas_call(
        functools.partial(kernel, n),
        out_shape=jax.ShapeDtypeStruct((n.cols, n.rows), f32),
        in_specs=[here, here, anywhere, anywhere, anywhere],
        out_specs=here,
        scratch_shapes=[
            vmem((3, n.exc, 2 * LANES), jnp.int32),
            vmem((3, LANES, 2 * LANES), jnp.int32),
            vmem((n.pair_pad, n.pair_pad), bf16),
            vmem((n.step * LANES, n.pair_pad), bf16),
            vmem(piece, f32),
            vmem(piece, bf16),
            vmem(piece, bf16),
            vmem((2, n.spots, *piece), bf16),
            vmem((2, 2, n.zs, *piece), bf16),
            vmem((n.strings, LANES), f32),
            vmem((2 * LANES, n.strings), bf16),
            vmem((total, n.strings), bf16),
            vmem((n.own, LANES, LANES), bf16),
            vmem((2 * LANES, total), bf16),
            vmem((2 * LANES, n.strings), f32),
            vmem((n.tiles, 2 * n.cols, LANES), f32),
            vmem((n.strings, LANES), bf16),
            vmem((n.strings, LANES), bf16),
            vmem((n.strings, LANES), bf16),
            vmem((n.tiles, 2 * n.cols, LANES), bf16),
            vmem((n.tiles, 2 * n.cols, LANES), bf16),
            vmem((n.zs, *piece), bf16),
            vmem((n.zs, *piece), bf16),
            vmem((n.zs, *piece), bf16),
            vmem((n.spots, *piece), bf16),
            vmem((n.zs, *piece), bf16),
            vmem(piece, f32),
            vmem(piece, f32),
            dma((3,)),
            dma((1,)),
            dma((1,)),
            dma((n.spots,)),
            dma((n.spots,)),
            dma((n.spots,)),
            dma((n.spots,)),
            dma((n.zs,)),
            dma((n.zs,)),
            dma((n.zs,)),
            dma((n.zs,)),
            dma((2, n.zs)),
            dma((2, n.zs)),
            dma((n.ys,)),
            dma((n.ys,)),
            dma((n.zs,)),
            dma((n.zs,)),
            dma((n.spots,)),
            dma((n.spots,)),
            dma((n.zs,)),
            dma((n.zs,)),
            dma((n.zs,)),
            dma((n.zs,)),
            dma((1,)),
            dma((1,)),
        ],
        compiler_params=pltpu.CompilerParams(
            collective_id=0, has_side_effects=True, vmem_limit_bytes=56 * 1024 * 1024
        ),
        name="sigma",
    )(coefficients.T, integrals, targets, orbital_pairs, phases)
    return sigma_t.T


def solution(mesh):
    in_specs = (P("tile", "wide"), P(), P(), P(), P())
    return jax.shard_map(
        functools.partial(per_device, mesh),
        mesh=mesh,
        in_specs=in_specs,
        out_specs=P("tile", "wide"),
        check_vma=False,
    )
```

```python
import functools
import types

import jax
import jax.numpy as jnp
from jax import lax
from jax.experimental import pallas as pl
from jax.experimental.pallas import tpu as pltpu
from jax.sharding import PartitionSpec as P

LANES = 128
MESH = pl.DeviceIdType.MESH


def plan_of(mesh, coef_shape, exc_shape, pair_count):
    tiles, wides = mesh.shape["tile"], mesh.shape["wide"]
    xs = 4 if wides == 32 else 2
    ys = wides // (2 * xs)
    zs = tiles // 2
    strings = coef_shape[0]
    ranges = strings // (3 * LANES)
    return types.SimpleNamespace(
        tiles=tiles,
        xs=xs,
        ys=ys,
        zs=zs,
        far=5 if zs == 8 else 1,
        spots=xs * ys,
        strings=strings,
        rows=strings // tiles,
        cols=strings // wides,
        own=strings // (xs * ys * 2),
        exc=exc_shape[0],
        pairs=pair_count,
        pair_pad=-(-pair_count // LANES) * LANES,
        step=8,
        ranges=ranges,
        order=sorted(range(ranges), key=lambda h: -abs(2 * h - ranges + 1)),
        width=strings // ranges,
    )


def kernel(n, coef, integ, tgt, prs, phs, out, raw, tabs, g_pad, p_part, c_pad, first, hold, gath_b, gath_a,
           xt, x_all, t_all, w_all, u_all, part, xa, sb, rb, ob, sa, ra, sx, rx, oa, in_b, in_c, in_a, fin, fin_in,
           s_tab, s1, r1, s2b, r2b, s5b, r5b, s2a, r2a, sxa, rxa, sxd, s5a, r5a, s6b, r6b, s6a, r6a,
           s3b, r3b, s3c, r3c, s7, r7, s8, r8, s4, r4):
    bf16, f32 = jnp.bfloat16, jnp.float32
    tile, wide = lax.axis_index("tile"), lax.axis_index("wide")
    core, zl = lax.rem(tile, 2), tile // 2
    x, zh, y = lax.rem(wide, n.xs), lax.rem(wide // n.xs, 2), wide // (2 * n.xs)
    spot = y * n.xs + x
    x_low, x_high = lax.rem(x, 2), x // 2

    def device(xx, yy, zzh, zzl, cc):
        return (zzl * 2 + cc, (yy * 2 + zzh) * n.xs + xx)

    def at_spot(j):
        return device(lax.rem(j, n.xs), j // n.xs, zh, zl, core)

    def on_line(z):
        return device(x, y, zh, z, core)

    def on_mates_line(z):
        return device(x_high * 2 + 1 - x_low, y, zh, z, core)

    def at_spot_over(j):
        return device(lax.rem(j, n.xs), j // n.xs, zh, zl, 1 - core)

    def is_far(z):
        return jnp.abs(z - zl) >= n.far

    def near_first(i):
        return jnp.where(zl < n.zs // 2, i, n.zs - 1 - i)

    def other(d):
        return lax.rem(spot + d, n.spots)

    def other_z(d):
        return lax.rem(zl + d, n.zs)

    partner = device(x, y, zh, zl, 1 - core)
    mate = device(x_high * 2 + 1 - x_low, y, zh, zl, core)
    half = n.zs // 2
    far_z = lax.rem(zl + half + n.zs * core, 2 * n.zs)
    far_out = device(x, y, far_z // n.zs, lax.rem(far_z, n.zs), zh)
    back_z = zh * n.zs + zl + 2 * n.zs - half
    back_zl = lax.rem(back_z, n.zs)
    far_in = device(x, y, core, back_zl, lax.rem(back_z - back_zl, 2 * n.zs) // n.zs)

    def remote(src, dst, send, recv, to):
        return pltpu.make_async_remote_copy(
            src_ref=src, dst_ref=dst, send_sem=send, recv_sem=recv, device_id=to, device_id_type=MESH
        )

    place = lax.rem(y * (n.xs // 2) + x_high + zl, n.zs)
    start = ((x_low * 2 + core) * n.zs + place) * n.own
    window = jnp.minimum(start // LANES * LANES, n.strings - 2 * LANES)
    window = pl.multiple_of(window, LANES)
    loads = [
        pltpu.make_async_copy(ref.at[:, pl.ds(window, 2 * LANES)], raw.at[i], s_tab.at[i])
        for i, ref in enumerate((tgt, prs, phs))
    ]
    for load in loads:
        load.start()

    barrier = pltpu.get_barrier_semaphore()

    def greet(whom):
        pl.semaphore_signal(barrier, inc=1, device_id=whom, device_id_type=MESH)

    def greet_line(d, carry):
        greet(on_line(other_z(d)))
        greet(on_mates_line(other_z(d)))
        return carry

    def greet_plane(d, carry):
        greet(at_spot(other(d)))
        greet(at_spot_over(other(d)))
        return carry

    greet(far_out)
    greet(far_in)
    lax.fori_loop(1, n.zs, greet_line, 0)
    lax.fori_loop(1, n.spots, greet_plane, 0)
    greet(partner)

    c_pad[...] = jnp.zeros_like(c_pad)
    c_pad[:, 0 : n.rows] = coef[...].astype(f32)
    first[...] = c_pad[...].astype(bf16)

    g_pad[...] = jnp.zeros_like(g_pad)
    g_pad[0 : n.pairs, 0 : n.pairs] = integ[...]
    tabs[...] = jnp.zeros_like(tabs)
    for load in loads:
        load.wait()
    tabs[:, 0 : n.exc] = raw[...]

    offset = start - window
    lane = lax.broadcasted_iota(jnp.int32, (LANES, LANES), 1).astype(f32).astype(bf16)
    one, zero = jnp.ones((), bf16), jnp.zeros((), bf16)

    def spread_col(col):
        return jnp.broadcast_to(col, (LANES, LANES)).astype(bf16)

    def build(it, carry):
        shift = lax.rem(2 * 2 * LANES - offset - it * n.step, 2 * LANES)
        t = pltpu.roll(tabs[0], shift, 1)[:, 0:LANES]
        q = pltpu.roll(tabs[1], shift, 1)[:, 0:LANES]
        s = pltpu.roll(tabs[2], shift, 1)[:, 0:LANES].astype(f32)
        t_hi, t_lo = (t // LANES).astype(f32), lax.rem(t, LANES).astype(f32)
        q_hi, q_lo = (q // LANES).astype(f32), lax.rem(q, LANES).astype(f32)
        for u in range(n.step):
            hi, lo = spread_col(q_hi[:, u : u + 1]), spread_col(q_lo[:, u : u + 1])
            sign = spread_col(s[:, u : u + 1])
            hot = jnp.where(lo == lane, sign, zero)
            for kt in range(n.pair_pad // LANES):
                p_part[u * LANES : (u + 1) * LANES, kt * LANES : (kt + 1) * LANES] = jnp.where(
                    hi == kt, hot, zero
                )
        picked = lax.dot_general(
            p_part[...], g_pad[...], (((1,), (1,)), ((), ())), preferred_element_type=f32
        ).astype(bf16)
        for u in range(n.step):
            b = it * n.step + u
            rows = pl.ds(pl.multiple_of(b * LANES, LANES), LANES)
            hi, lo = spread_col(t_hi[:, u : u + 1]), spread_col(t_lo[:, u : u + 1])
            hot = jnp.where(lo == lane, one, zero)
            for kt in range(n.strings // LANES):
                t_all[rows, kt * LANES : (kt + 1) * LANES] = jnp.where(hi == kt, hot, zero)
        for u in range(n.step):
            rows = slice(u * LANES, (u + 1) * LANES)
            w_all[it * n.step + u] = lax.dot_general(
                picked[rows], p_part[rows], (((1,), (1,)), ((), ())), preferred_element_type=f32
            ).astype(bf16)
        return carry

    builds = n.own // n.step
    cuts = [0, builds // 3, builds * 2 // 3, builds * 5 // 6, builds]

    pl.semaphore_wait(barrier, 2 + 2 * (n.zs - 1) + 2 * (n.spots - 1) + 1)

    def line(to, frm):
        return remote(first, gath_a.at[core, x_low, frm], s2a.at[to], r2a.at[frm], on_line(to))

    def line_over(to):
        return remote(first, gath_a.at[core, x_low, zl], sxd.at[to], rxa.at[zl], on_mates_line(to))

    def to_mate(z, side):
        ref = gath_a.at[core, side, z]
        return remote(ref, ref, sxa.at[z], rxa.at[z], mate)

    def relay_a(z, side, cc):
        ref = gath_a.at[cc, side, z]
        return remote(ref, ref, s5a.at[side, z], r5a.at[side, z], partner)

    def share(to, frm):
        return remote(hold, gath_b.at[core, frm], s2b.at[to], r2b.at[frm], at_spot(to))

    def relay_b(j, cc):
        ref = gath_b.at[cc, j]
        return remote(ref, ref, s5b.at[j], r5b.at[j], partner)

    forth = remote(first, hold, s1.at[0], r1.at[0], far_out)
    forth.start()

    def start_line(i, carry):
        z = near_first(n.zs - 1 - i)

        @pl.when(z != zl)
        def _():
            line(z, zl).start()

        @pl.when(is_far(z))
        def _():
            line_over(z).start()

        return carry

    lax.fori_loop(0, n.zs, start_line, 0)
    gath_a[core, x_low, zl] = first[...]
    to_mate(zl, x_low).start()
    relay_a(zl, x_low, core).start()

    lax.fori_loop(cuts[0], cuts[1], build, 0)

    forth.wait_recv()

    def start_share(d, carry):
        share(other(d), spot).start()
        return carry

    lax.fori_loop(1, n.spots, start_share, 0)
    gath_b[core, spot] = hold[...]
    relay_b(spot, core).start()

    lax.fori_loop(cuts[1], cuts[2], build, 0)

    def hand_line(i, carry):
        z = near_first(i)

        @pl.when(z != zl)
        def _():
            line(zl, z).wait_recv()

            @pl.when(jnp.logical_not(is_far(z)))
            def _():
                to_mate(z, x_low).start()

            relay_a(z, x_low, core).start()

        return carry

    lax.fori_loop(0, n.zs, hand_line, 0)
    lax.fori_loop(cuts[2], cuts[3], build, 0)

    def hand_plane(d, carry):
        j = other(d)
        share(spot, j).wait_recv()
        relay_b(j, core).start()
        return carry

    lax.fori_loop(1, n.spots, hand_plane, 0)

    def hand_mate(i, carry):
        z = near_first(i)
        to_mate(z, 1 - x_low).wait_recv()
        relay_a(z, 1 - x_low, core).start()
        return carry

    lax.fori_loop(0, n.zs, hand_mate, 0)
    lax.fori_loop(cuts[3], cuts[4], build, 0)

    def wait_relay_b(j, carry):
        relay_b(j, 1 - core).wait_recv()
        return carry

    lax.fori_loop(0, n.spots, wait_relay_b, 0)

    for w in range(2 * n.spots):
        yy, cc, xx = w // (2 * n.xs), w // n.xs % 2, w % n.xs
        xt[w * n.cols : (w + 1) * n.cols] = gath_b[cc, yy * n.xs + xx].astype(f32)
    for kt in range(n.strings // LANES):
        at = slice(kt * LANES, (kt + 1) * LANES)
        x_all[0:LANES, at] = xt[at].T.astype(bf16)

    def wait_relay_a(z, carry):
        relay_a(z, 0, 1 - core).wait_recv()
        relay_a(z, 1, 1 - core).wait_recv()
        return carry

    lax.fori_loop(0, n.zs, wait_relay_a, 0)

    lane_i = lax.broadcasted_iota(jnp.int32, (LANES, LANES), 1)
    spare = jnp.zeros((LANES - 2 * n.cols, LANES), f32)

    def alpha_piece(t):
        low, high = (gath_a[t % 2, side, t // 2].astype(f32) for side in range(2))
        return jnp.concatenate([low, high, spare], axis=0)

    for four in range(n.tiles // 4):
        p0, p1, p2, p3 = (alpha_piece(4 * four + i) for i in range(4))
        p1, p2, p3 = pltpu.roll(p1, 96, 1), pltpu.roll(p2, 64, 1), pltpu.roll(p3, 32, 1)
        tiles3 = (
            jnp.where(lane_i < 96, p0, p1),
            jnp.where(lane_i < 64, p1, p2),
            jnp.where(lane_i < 32, p2, p3),
        )
        for i, value in enumerate(tiles3):
            at = (3 * four + i) * LANES
            x_all[LANES : 2 * LANES, at : at + LANES] = value.astype(bf16)

    many = min(8, n.own)

    def couple(it, carry):
        rows = pl.ds(pl.multiple_of(it * many * LANES, many * LANES), many * LANES)
        v = lax.dot_general(
            x_all[...], t_all[rows, :], (((1,), (1,)), ((), ())), preferred_element_type=f32
        ).astype(bf16)
        for u in range(many):
            value = jnp.dot(
                v[:, u * LANES : (u + 1) * LANES], w_all[it * many + u], preferred_element_type=f32
            )
            at = pl.ds(pl.multiple_of((it * many + u) * LANES, LANES), LANES)
            u_all[:, at] = value.astype(bf16)
        return carry

    lax.fori_loop(0, n.own // many, couple, 0)

    block = n.xs * n.cols
    keep = pl.ds(pl.multiple_of(x_low * n.cols, 16), n.cols)
    pass_on = pl.ds(pl.multiple_of((1 - x_low) * n.cols, 16), n.cols)

    def block_rows(yy, cc):
        return pl.ds(pl.multiple_of((yy * 2 + cc) * block, 16), block)

    def ys_of(h):
        return range(h * n.ys // n.ranges, (h + 1) * n.ys // n.ranges)

    def zs_of(h):
        return range(h * n.zs // n.ranges, (h + 1) * n.zs // n.ranges)

    def cross_b(yy, cc):
        rows = block_rows(yy, cc)
        return remote(sb.at[rows], rb.at[rows], s6b.at[yy], r6b.at[yy], partner)

    def cross_a(z, cc):
        return remote(sa.at[2 * z + cc], ra.at[2 * z + cc], s6a.at[z], r6a.at[z], partner)

    def across(z):
        return remote(sx.at[z], rx.at[z], s7.at[z], r7.at[z], mate)

    def down_line(to, frm):
        return remote(oa.at[to], in_a.at[frm], s8.at[to], r8.at[frm], on_line(to))

    def to_plane(rows, to, frm):
        return remote(ob.at[rows], in_b.at[frm], s3b.at[to], r3b.at[frm], at_spot(to))

    def to_plane_over(rows, to, frm):
        return remote(ob.at[rows], in_c.at[frm], s3c.at[to], r3c.at[frm], at_spot_over(to))

    def piece_rows(yy, cc, xx):
        return pl.ds(pl.multiple_of(((yy * 2 + cc) * n.xs + xx) * n.cols, 16), n.cols)

    last = n.order[-1]

    def scatter(h):
        at = slice(h * n.width, (h + 1) * n.width)
        part[:, at] = jnp.dot(u_all[...], t_all[:, at], preferred_element_type=f32)

    def sum_cores(h):
        for kt in range(3 * h, 3 * h + 3):
            at = slice(kt * LANES, (kt + 1) * LANES)
            xt[at] = part[0:LANES, at].T
        for yy in ys_of(h):
            if h == last:
                rows = pl.ds(yy * 2 * block, 2 * block)
                ob[rows] = xt[rows].astype(bf16)
                for i in range(n.xs):
                    xx = lax.rem(x + i, n.xs)
                    to_plane_over(piece_rows(yy, 1 - core, xx), yy * n.xs + xx, spot).start()

                    @pl.when(jnp.logical_or(xx != x, y != yy))
                    def _():
                        to_plane(piece_rows(yy, core, xx), yy * n.xs + xx, spot).start()

            else:
                rows = block_rows(yy, 1 - core)
                sb[rows] = xt[rows].astype(bf16)
                cross_b(yy, 1 - core).start()
        t0, t1, t2 = (
            part[LANES : 2 * LANES, (3 * h + i) * LANES : (3 * h + i + 1) * LANES] for i in range(3)
        )
        roll = functools.partial(pltpu.roll, axis=1)
        values = (
            t0,
            jnp.where(lane_i < 32, roll(t0, 32), roll(t1, 32)),
            jnp.where(lane_i < 64, roll(t1, 64), roll(t2, 64)),
            roll(t2, 96),
        )
        for i, value in enumerate(values):
            xa[4 * h + i] = value[0 : 2 * n.cols]
        for z in zs_of(h):
            sa[2 * z + 1 - core] = xa[2 * z + 1 - core].astype(bf16)
            cross_a(z, 1 - core).start()

    def sum_mates(h):
        for yy in ys_of(h) if h != last else ():
            rows = block_rows(yy, core)
            cross_b(yy, core).wait_recv()
            total = xt[rows] + rb[rows].astype(f32)
            xt[rows] = total
            ob[rows] = total.astype(bf16)
            for i in range(n.xs):
                xx = lax.rem(x + i, n.xs)

                @pl.when(jnp.logical_or(xx != x, y != yy))
                def _():
                    to_plane(piece_rows(yy, core, xx), yy * n.xs + xx, spot).start()

        for z in zs_of(h):
            cross_a(z, core).wait_recv()
            xa[2 * z + core] = xa[2 * z + core] + ra[2 * z + core].astype(f32)
            sx[z] = xa[2 * z + core, pass_on].astype(bf16)
            across(z).start()

    def sum_line(h):
        for z in zs_of(h):
            across(z).wait_recv()
            total = xa[2 * z + core, keep] + rx[z].astype(f32)
            xa[2 * z + core, keep] = total
            oa[z] = total.astype(bf16)

            @pl.when(z != zl)
            def _():
                down_line(z, zl).start()

    for i in range(n.ranges + 2):
        if i < n.ranges:
            scatter(n.order[i])
        if 0 <= i - 2 < n.ranges:
            sum_line(n.order[i - 2])
        if 0 <= i - 1 < n.ranges:
            sum_mates(n.order[i - 1])
        if i < n.ranges:
            sum_cores(n.order[i])

    fin[...] = xt[piece_rows(y, core, x)]

    def add_plane(d, carry):
        j = other(d)
        to_plane(pl.ds(0, n.cols), spot, j).wait_recv()
        fin[...] += in_b[j].astype(f32)
        return carry

    lax.fori_loop(1, n.spots, add_plane, 0)

    def add_over(j, carry):
        to_plane_over(pl.ds(0, n.cols), spot, j).wait_recv()
        fin[...] += in_c[j].astype(f32)
        return carry

    @pl.when((y >= ys_of(last)[0]) & (y <= ys_of(last)[-1]))
    def _():
        lax.fori_loop(0, n.spots, add_over, 0)

    back = remote(fin, fin_in, s4.at[0], r4.at[0], far_in)
    back.start()

    c_pad[...] = xa[2 * zl + core, keep]

    def add_line(d, carry):
        z = other_z(d)
        down_line(zl, z).wait_recv()
        c_pad[...] += in_a[z].astype(f32)
        return carry

    lax.fori_loop(1, n.zs, add_line, 0)

    forth.wait_send()

    def drain_line(d, carry):
        z = other_z(d)
        line(z, zl).wait_send()
        down_line(z, zl).wait_send()

        @pl.when(is_far(z))
        def _():
            line_over(z).wait_send()

        return carry

    lax.fori_loop(1, n.zs, drain_line, 0)

    def drain_line_all(z, carry):
        @pl.when(jnp.logical_not(is_far(z)))
        def _():
            to_mate(z, x_low).wait_send()

        relay_a(z, 0, core).wait_send()
        relay_a(z, 1, core).wait_send()
        cross_a(z, 1 - core).wait_send()
        across(z).wait_send()
        return carry

    lax.fori_loop(0, n.zs, drain_line_all, 0)

    def drain_plane(d, carry):
        j = other(d)
        share(j, spot).wait_send()
        to_plane(pl.ds(0, n.cols), j, spot).wait_send()
        return carry

    lax.fori_loop(1, n.spots, drain_plane, 0)

    def drain_plane_all(j, carry):
        relay_b(j, core).wait_send()
        return carry

    lax.fori_loop(0, n.spots, drain_plane_all, 0)
    for yy in range(n.ys):
        if yy not in ys_of(last):
            cross_b(yy, 1 - core).wait_send()
            continue
        for xx in range(n.xs):
            to_plane_over(pl.ds(0, n.cols), yy * n.xs + xx, spot).wait_send()

    back.wait_recv()
    out[...] = c_pad[:, 0 : n.rows] + fin_in[:, 0 : n.rows]
    back.wait_send()


def per_device(mesh, coefficients, integrals, targets, orbital_pairs, phases):
    rows, cols = coefficients.shape
    n = plan_of(
        mesh, (rows * mesh.shape["tile"], cols * mesh.shape["wide"]), targets.shape, integrals.shape[0]
    )
    bf16, f32 = jnp.bfloat16, jnp.float32
    total = n.own * LANES
    piece = (n.cols, LANES)
    dma, vmem = pltpu.SemaphoreType.DMA, pltpu.VMEM
    here, anywhere = pl.BlockSpec(memory_space=pltpu.VMEM), pl.BlockSpec(memory_space=pl.ANY)
    sigma_t = pl.pallas_call(
        functools.partial(kernel, n),
        out_shape=jax.ShapeDtypeStruct((n.cols, n.rows), f32),
        in_specs=[here, here, anywhere, anywhere, anywhere],
        out_specs=here,
        scratch_shapes=[
            vmem((3, n.exc, 2 * LANES), jnp.int32),
            vmem((3, LANES, 2 * LANES), jnp.int32),
            vmem((n.pair_pad, n.pair_pad), bf16),
            vmem((n.step * LANES, n.pair_pad), bf16),
            vmem(piece, f32),
            vmem(piece, bf16),
            vmem(piece, bf16),
            vmem((2, n.spots, *piece), bf16),
            vmem((2, 2, n.zs, *piece), bf16),
            vmem((n.strings, LANES), f32),
            vmem((2 * LANES, n.strings), bf16),
            vmem((total, n.strings), bf16),
            vmem((n.own, LANES, LANES), bf16),
            vmem((2 * LANES, total), bf16),
            vmem((2 * LANES, n.strings), f32),
            vmem((n.tiles, 2 * n.cols, LANES), f32),
            vmem((n.strings, LANES), bf16),
            vmem((n.strings, LANES), bf16),
            vmem((n.strings, LANES), bf16),
            vmem((n.tiles, 2 * n.cols, LANES), bf16),
            vmem((n.tiles, 2 * n.cols, LANES), bf16),
            vmem((n.zs, *piece), bf16),
            vmem((n.zs, *piece), bf16),
            vmem((n.zs, *piece), bf16),
            vmem((n.spots, *piece), bf16),
            vmem((n.spots, *piece), bf16),
            vmem((n.zs, *piece), bf16),
            vmem(piece, f32),
            vmem(piece, f32),
            dma((3,)),
            dma((1,)),
            dma((1,)),
            dma((n.spots,)),
            dma((n.spots,)),
            dma((n.spots,)),
            dma((n.spots,)),
            dma((n.zs,)),
            dma((n.zs,)),
            dma((n.zs,)),
            dma((n.zs,)),
            dma((n.zs,)),
            dma((2, n.zs)),
            dma((2, n.zs)),
            dma((n.ys,)),
            dma((n.ys,)),
            dma((n.zs,)),
            dma((n.zs,)),
            dma((n.spots,)),
            dma((n.spots,)),
            dma((n.spots,)),
            dma((n.spots,)),
            dma((n.zs,)),
            dma((n.zs,)),
            dma((n.zs,)),
            dma((n.zs,)),
            dma((1,)),
            dma((1,)),
        ],
        compiler_params=pltpu.CompilerParams(
            collective_id=0, has_side_effects=True, vmem_limit_bytes=56 * 1024 * 1024
        ),
        name="sigma",
    )(coefficients.T, integrals, targets, orbital_pairs, phases)
    return sigma_t.T


def solution(mesh):
    in_specs = (P("tile", "wide"), P(), P(), P(), P())
    return jax.shard_map(
        functools.partial(per_device, mesh),
        mesh=mesh,
        in_specs=in_specs,
        out_specs=P("tile", "wide"),
        check_vma=False,
    )
```

```python
import functools
import types

import jax
import jax.numpy as jnp
from jax import lax
from jax.experimental import pallas as pl
from jax.experimental.pallas import tpu as pltpu
from jax.sharding import PartitionSpec as P

LANES = 128
MESH = pl.DeviceIdType.MESH


def plan_of(mesh, coef_shape, exc_shape, pair_count):
    tiles, wides = mesh.shape["tile"], mesh.shape["wide"]
    xs = 4 if wides == 32 else 2
    ys = wides // (2 * xs)
    zs = tiles // 2
    strings = coef_shape[0]
    ranges = strings // (3 * LANES)
    return types.SimpleNamespace(
        tiles=tiles,
        xs=xs,
        ys=ys,
        zs=zs,
        group=zs // 2,
        spots=xs * ys,
        strings=strings,
        rows=strings // tiles,
        cols=strings // wides,
        own=strings // (xs * ys * 2),
        exc=exc_shape[0],
        pairs=pair_count,
        pair_pad=-(-pair_count // LANES) * LANES,
        step=8,
        ranges=ranges,
        order=sorted(range(ranges), key=lambda h: -abs(2 * h - ranges + 1)),
        width=strings // ranges,
    )


def kernel(n, coef, integ, tgt, prs, phs, out, raw, tabs, g_pad, p_part, c_pad, first, hold, gath_b, gath_a,
           xt, x_all, t_all, w_all, u_all, part, xa, sb, rb, ob, sa, ra, sx, rx, oa, in_b, in_c, in_a, fin, fin_in,
           s_tab, s1, r1, s2b, r2b, s5b, r5b, s2a, r2a, sxa, rxa, s2f, s2g, s5a, r5a, s6b, r6b, s6a, r6a,
           s3b, r3b, s3c, r3c, s7, r7, s8, r8, s4, r4):
    bf16, f32 = jnp.bfloat16, jnp.float32
    tile, wide = lax.axis_index("tile"), lax.axis_index("wide")
    core, zl = lax.rem(tile, 2), tile // 2
    x, zh, y = lax.rem(wide, n.xs), lax.rem(wide // n.xs, 2), wide // (2 * n.xs)
    spot = y * n.xs + x
    x_low, x_high = lax.rem(x, 2), x // 2

    def device(xx, yy, zzh, zzl, cc):
        return (zzl * 2 + cc, (yy * 2 + zzh) * n.xs + xx)

    def at_spot(j):
        return device(lax.rem(j, n.xs), j // n.xs, zh, zl, core)

    def on_line(z):
        return device(x, y, zh, z, core)

    def on_mates_line(z):
        return device(x_high * 2 + 1 - x_low, y, zh, z, core)

    def at_spot_over(j):
        return device(lax.rem(j, n.xs), j // n.xs, zh, zl, 1 - core)

    def near_z(d):
        return zl // n.group * n.group + lax.rem(zl + d, n.group)

    def across_z(z):
        return lax.rem(z + n.group, n.zs)

    def other(d):
        return lax.rem(spot + d, n.spots)

    def other_z(d):
        return lax.rem(zl + d, n.zs)

    partner = device(x, y, zh, zl, 1 - core)
    mate = device(x_high * 2 + 1 - x_low, y, zh, zl, core)
    half = n.zs // 2
    far_z = lax.rem(zl + half + n.zs * core, 2 * n.zs)
    far_out = device(x, y, far_z // n.zs, lax.rem(far_z, n.zs), zh)
    back_z = zh * n.zs + zl + 2 * n.zs - half
    back_zl = lax.rem(back_z, n.zs)
    far_in = device(x, y, core, back_zl, lax.rem(back_z - back_zl, 2 * n.zs) // n.zs)

    def remote(src, dst, send, recv, to):
        return pltpu.make_async_remote_copy(
            src_ref=src, dst_ref=dst, send_sem=send, recv_sem=recv, device_id=to, device_id_type=MESH
        )

    place = lax.rem(y * (n.xs // 2) + x_high + zl, n.zs)
    start = ((x_low * 2 + core) * n.zs + place) * n.own
    window = jnp.minimum(start // LANES * LANES, n.strings - 2 * LANES)
    window = pl.multiple_of(window, LANES)
    loads = [
        pltpu.make_async_copy(ref.at[:, pl.ds(window, 2 * LANES)], raw.at[i], s_tab.at[i])
        for i, ref in enumerate((tgt, prs, phs))
    ]
    for load in loads:
        load.start()

    barrier = pltpu.get_barrier_semaphore()

    def greet(whom):
        pl.semaphore_signal(barrier, inc=1, device_id=whom, device_id_type=MESH)

    def greet_line(d, carry):
        greet(on_line(other_z(d)))
        return carry

    def greet_plane(d, carry):
        greet(at_spot(other(d)))
        greet(at_spot_over(other(d)))
        return carry

    greet(far_out)
    greet(far_in)
    def greet_mates(d, carry):
        greet(on_mates_line(near_z(d)))
        return carry

    lax.fori_loop(1, n.zs, greet_line, 0)
    lax.fori_loop(1, n.group, greet_mates, 0)
    lax.fori_loop(1, n.spots, greet_plane, 0)
    greet(partner)

    c_pad[...] = jnp.zeros_like(c_pad)
    c_pad[:, 0 : n.rows] = coef[...].astype(f32)
    first[...] = c_pad[...].astype(bf16)

    g_pad[...] = jnp.zeros_like(g_pad)
    g_pad[0 : n.pairs, 0 : n.pairs] = integ[...]
    tabs[...] = jnp.zeros_like(tabs)
    for load in loads:
        load.wait()
    tabs[:, 0 : n.exc] = raw[...]

    offset = start - window
    lane = lax.broadcasted_iota(jnp.int32, (LANES, LANES), 1).astype(f32).astype(bf16)
    one, zero = jnp.ones((), bf16), jnp.zeros((), bf16)

    def spread_col(col):
        return jnp.broadcast_to(col, (LANES, LANES)).astype(bf16)

    def build(it, carry):
        shift = lax.rem(2 * 2 * LANES - offset - it * n.step, 2 * LANES)
        t = pltpu.roll(tabs[0], shift, 1)[:, 0:LANES]
        q = pltpu.roll(tabs[1], shift, 1)[:, 0:LANES]
        s = pltpu.roll(tabs[2], shift, 1)[:, 0:LANES].astype(f32)
        t_hi, t_lo = (t // LANES).astype(f32), lax.rem(t, LANES).astype(f32)
        q_hi, q_lo = (q // LANES).astype(f32), lax.rem(q, LANES).astype(f32)
        for u in range(n.step):
            hi, lo = spread_col(q_hi[:, u : u + 1]), spread_col(q_lo[:, u : u + 1])
            sign = spread_col(s[:, u : u + 1])
            hot = jnp.where(lo == lane, sign, zero)
            for kt in range(n.pair_pad // LANES):
                p_part[u * LANES : (u + 1) * LANES, kt * LANES : (kt + 1) * LANES] = jnp.where(
                    hi == kt, hot, zero
                )
        picked = lax.dot_general(
            p_part[...], g_pad[...], (((1,), (1,)), ((), ())), preferred_element_type=f32
        ).astype(bf16)
        for u in range(n.step):
            b = it * n.step + u
            rows = pl.ds(pl.multiple_of(b * LANES, LANES), LANES)
            hi, lo = spread_col(t_hi[:, u : u + 1]), spread_col(t_lo[:, u : u + 1])
            hot = jnp.where(lo == lane, one, zero)
            for kt in range(n.strings // LANES):
                t_all[rows, kt * LANES : (kt + 1) * LANES] = jnp.where(hi == kt, hot, zero)
        for u in range(n.step):
            rows = slice(u * LANES, (u + 1) * LANES)
            w_all[it * n.step + u] = lax.dot_general(
                picked[rows], p_part[rows], (((1,), (1,)), ((), ())), preferred_element_type=f32
            ).astype(bf16)
        return carry

    builds = n.own // n.step
    early = builds * 2 // 3

    lax.fori_loop(0, early, build, 0)
    pl.semaphore_wait(barrier, 2 + n.zs - 1 + n.group - 1 + 2 * (n.spots - 1) + 1)

    def line(to, frm):
        return remote(first, gath_a.at[core, x_low, frm], s2a.at[to], r2a.at[frm], on_line(to))

    def line_on(to, frm):
        ref = gath_a.at[core, x_low, frm]
        return remote(ref, ref, s2f.at[to], r2a.at[frm], on_line(to))

    def line_over(to, frm):
        ref = gath_a.at[core, x_low, frm]
        return remote(ref, ref, s2g.at[to], rxa.at[frm], on_mates_line(to))

    def to_mate(z, side):
        ref = gath_a.at[core, side, z]
        return remote(ref, ref, sxa.at[z], rxa.at[z], mate)

    def relay_a(z, side, cc):
        ref = gath_a.at[cc, side, z]
        return remote(ref, ref, s5a.at[side, z], r5a.at[side, z], partner)

    def share(to, frm):
        return remote(hold, gath_b.at[core, frm], s2b.at[to], r2b.at[frm], at_spot(to))

    def relay_b(j, cc):
        ref = gath_b.at[cc, j]
        return remote(ref, ref, s5b.at[j], r5b.at[j], partner)

    forth = remote(first, hold, s1.at[0], r1.at[0], far_out)
    forth.start()

    def start_line(d, carry):
        line(near_z(d), zl).start()
        return carry

    line(across_z(zl), zl).start()
    lax.fori_loop(1, n.group, start_line, 0)
    gath_a[core, x_low, zl] = first[...]
    to_mate(zl, x_low).start()
    relay_a(zl, x_low, core).start()

    lax.fori_loop(early, builds, build, 0)

    line(zl, across_z(zl)).wait_recv()

    def start_line_on(d, carry):
        line_on(near_z(d), across_z(zl)).start()
        line_over(near_z(d), across_z(zl)).start()
        return carry

    lax.fori_loop(1, n.group, start_line_on, 0)
    to_mate(across_z(zl), x_low).start()
    relay_a(across_z(zl), x_low, core).start()

    forth.wait_recv()

    def start_share(d, carry):
        share(other(d), spot).start()
        return carry

    lax.fori_loop(1, n.spots, start_share, 0)
    gath_b[core, spot] = hold[...]
    relay_b(spot, core).start()

    def hand_line(d, carry):
        z = near_z(d)
        line(zl, z).wait_recv()
        to_mate(z, x_low).start()
        relay_a(z, x_low, core).start()
        return carry

    lax.fori_loop(1, n.group, hand_line, 0)

    def hand_line_on(d, carry):
        z = across_z(near_z(d))
        line(zl, z).wait_recv()
        relay_a(z, x_low, core).start()
        return carry

    lax.fori_loop(1, n.group, hand_line_on, 0)

    def hand_plane(d, carry):
        j = other(d)
        share(spot, j).wait_recv()
        relay_b(j, core).start()
        return carry

    lax.fori_loop(1, n.spots, hand_plane, 0)

    def hand_mate(d, carry):
        z = other_z(d)
        to_mate(z, 1 - x_low).wait_recv()
        relay_a(z, 1 - x_low, core).start()
        return carry

    lax.fori_loop(0, n.zs, hand_mate, 0)

    def wait_relay_b(j, carry):
        relay_b(j, 1 - core).wait_recv()
        return carry

    lax.fori_loop(0, n.spots, wait_relay_b, 0)

    for w in range(2 * n.spots):
        yy, cc, xx = w // (2 * n.xs), w // n.xs % 2, w % n.xs
        xt[w * n.cols : (w + 1) * n.cols] = gath_b[cc, yy * n.xs + xx].astype(f32)
    for kt in range(n.strings // LANES):
        at = slice(kt * LANES, (kt + 1) * LANES)
        x_all[0:LANES, at] = xt[at].T.astype(bf16)

    def wait_relay_a(z, carry):
        relay_a(z, 0, 1 - core).wait_recv()
        relay_a(z, 1, 1 - core).wait_recv()
        return carry

    lax.fori_loop(0, n.zs, wait_relay_a, 0)

    lane_i = lax.broadcasted_iota(jnp.int32, (LANES, LANES), 1)
    spare = jnp.zeros((LANES - 2 * n.cols, LANES), f32)

    def alpha_piece(t):
        low, high = (gath_a[t % 2, side, t // 2].astype(f32) for side in range(2))
        return jnp.concatenate([low, high, spare], axis=0)

    for four in range(n.tiles // 4):
        p0, p1, p2, p3 = (alpha_piece(4 * four + i) for i in range(4))
        p1, p2, p3 = pltpu.roll(p1, 96, 1), pltpu.roll(p2, 64, 1), pltpu.roll(p3, 32, 1)
        tiles3 = (
            jnp.where(lane_i < 96, p0, p1),
            jnp.where(lane_i < 64, p1, p2),
            jnp.where(lane_i < 32, p2, p3),
        )
        for i, value in enumerate(tiles3):
            at = (3 * four + i) * LANES
            x_all[LANES : 2 * LANES, at : at + LANES] = value.astype(bf16)

    many = min(8, n.own)

    def couple(it, carry):
        rows = pl.ds(pl.multiple_of(it * many * LANES, many * LANES), many * LANES)
        v = lax.dot_general(
            x_all[...], t_all[rows, :], (((1,), (1,)), ((), ())), preferred_element_type=f32
        ).astype(bf16)
        for u in range(many):
            value = jnp.dot(
                v[:, u * LANES : (u + 1) * LANES], w_all[it * many + u], preferred_element_type=f32
            )
            at = pl.ds(pl.multiple_of((it * many + u) * LANES, LANES), LANES)
            u_all[:, at] = value.astype(bf16)
        return carry

    lax.fori_loop(0, n.own // many, couple, 0)

    block = n.xs * n.cols
    keep = pl.ds(pl.multiple_of(x_low * n.cols, 16), n.cols)
    pass_on = pl.ds(pl.multiple_of((1 - x_low) * n.cols, 16), n.cols)

    def block_rows(yy, cc):
        return pl.ds(pl.multiple_of((yy * 2 + cc) * block, 16), block)

    def ys_of(h):
        return range(h * n.ys // n.ranges, (h + 1) * n.ys // n.ranges)

    def zs_of(h):
        return range(h * n.zs // n.ranges, (h + 1) * n.zs // n.ranges)

    def cross_b(yy, cc):
        rows = block_rows(yy, cc)
        return remote(sb.at[rows], rb.at[rows], s6b.at[yy], r6b.at[yy], partner)

    def cross_a(z, cc):
        return remote(sa.at[2 * z + cc], ra.at[2 * z + cc], s6a.at[z], r6a.at[z], partner)

    def across(z):
        return remote(sx.at[z], rx.at[z], s7.at[z], r7.at[z], mate)

    def down_line(to, frm):
        return remote(oa.at[to], in_a.at[frm], s8.at[to], r8.at[frm], on_line(to))

    def to_plane(rows, to, frm):
        return remote(ob.at[rows], in_b.at[frm], s3b.at[to], r3b.at[frm], at_spot(to))

    def to_plane_over(rows, to, frm):
        return remote(ob.at[rows], in_c.at[frm], s3c.at[to], r3c.at[frm], at_spot_over(to))

    def piece_rows(yy, cc, xx):
        return pl.ds(pl.multiple_of(((yy * 2 + cc) * n.xs + xx) * n.cols, 16), n.cols)

    last = n.order[-1]

    def scatter(h):
        at = slice(h * n.width, (h + 1) * n.width)
        part[:, at] = jnp.dot(u_all[...], t_all[:, at], preferred_element_type=f32)

    def sum_cores(h):
        t0, t1, t2 = (
            part[LANES : 2 * LANES, (3 * h + i) * LANES : (3 * h + i + 1) * LANES] for i in range(3)
        )
        roll = functools.partial(pltpu.roll, axis=1)
        values = (
            t0,
            jnp.where(lane_i < 32, roll(t0, 32), roll(t1, 32)),
            jnp.where(lane_i < 64, roll(t1, 64), roll(t2, 64)),
            roll(t2, 96),
        )
        for i, value in enumerate(values):
            xa[4 * h + i] = value[0 : 2 * n.cols]
        for z in zs_of(h):
            sa[2 * z + 1 - core] = xa[2 * z + 1 - core].astype(bf16)
            cross_a(z, 1 - core).start()
        for kt in range(3 * h, 3 * h + 3):
            at = slice(kt * LANES, (kt + 1) * LANES)
            xt[at] = part[0:LANES, at].T
        for yy in ys_of(h):
            if h == last:
                rows = pl.ds(yy * 2 * block, 2 * block)
                ob[rows] = xt[rows].astype(bf16)
                for i in range(n.xs):
                    xx = lax.rem(x + i, n.xs)
                    to_plane_over(piece_rows(yy, 1 - core, xx), yy * n.xs + xx, spot).start()

                    @pl.when(jnp.logical_or(xx != x, y != yy))
                    def _():
                        to_plane(piece_rows(yy, core, xx), yy * n.xs + xx, spot).start()

            else:
                rows = block_rows(yy, 1 - core)
                sb[rows] = xt[rows].astype(bf16)
                cross_b(yy, 1 - core).start()

    def sum_mates(h):
        for z in zs_of(h):
            cross_a(z, core).wait_recv()
            xa[2 * z + core] = xa[2 * z + core] + ra[2 * z + core].astype(f32)
            sx[z] = xa[2 * z + core, pass_on].astype(bf16)
            across(z).start()
        for yy in ys_of(h) if h != last else ():
            rows = block_rows(yy, core)
            cross_b(yy, core).wait_recv()
            total = xt[rows] + rb[rows].astype(f32)
            xt[rows] = total
            ob[rows] = total.astype(bf16)
            for i in range(n.xs):
                xx = lax.rem(x + i, n.xs)

                @pl.when(jnp.logical_or(xx != x, y != yy))
                def _():
                    to_plane(piece_rows(yy, core, xx), yy * n.xs + xx, spot).start()

    def sum_line(h):
        for z in zs_of(h):
            across(z).wait_recv()
            total = xa[2 * z + core, keep] + rx[z].astype(f32)
            xa[2 * z + core, keep] = total
            oa[z] = total.astype(bf16)

            @pl.when(z != zl)
            def _():
                down_line(z, zl).start()

    for i in range(n.ranges + 2):
        if i < n.ranges:
            scatter(n.order[i])
        if 0 <= i - 2 < n.ranges:
            sum_line(n.order[i - 2])
        if 0 <= i - 1 < n.ranges:
            sum_mates(n.order[i - 1])
        if i < n.ranges:
            sum_cores(n.order[i])

    in_b[spot] = jnp.zeros_like(first)

    def wait_plane(d, carry):
        to_plane(pl.ds(0, n.cols), spot, other(d)).wait_recv()
        return carry

    def wait_over(j, carry):
        to_plane_over(pl.ds(0, n.cols), spot, j).wait_recv()
        return carry

    def total_of(ref, count):
        terms = [ref[j].astype(f32) for j in range(count)]
        while len(terms) > 1:
            terms = [a + b for a, b in zip(terms[::2], terms[1::2])] + terms[len(terms) & ~1 :]
        return terms[0]

    in_last = (y >= ys_of(last)[0]) & (y <= ys_of(last)[-1])
    lax.fori_loop(1, n.spots, wait_plane, 0)
    fin[...] = xt[piece_rows(y, core, x)] + total_of(in_b, n.spots)

    @pl.when(in_last)
    def _():
        lax.fori_loop(0, n.spots, wait_over, 0)
        fin[...] += total_of(in_c, n.spots)

    back = remote(fin, fin_in, s4.at[0], r4.at[0], far_in)
    back.start()

    in_a[zl] = jnp.zeros_like(first)

    def wait_line(d, carry):
        down_line(zl, other_z(d)).wait_recv()
        return carry

    lax.fori_loop(1, n.zs, wait_line, 0)
    c_pad[...] = xa[2 * zl + core, keep] + total_of(in_a, n.zs)

    forth.wait_send()

    def drain_line(d, carry):
        down_line(other_z(d), zl).wait_send()
        return carry

    def drain_near(d, carry):
        z = near_z(d)
        line(z, zl).wait_send()
        line_on(z, zl).wait_send()
        line_over(z, zl).wait_send()
        to_mate(z, x_low).wait_send()
        return carry

    def drain_line_all(z, carry):
        relay_a(z, 0, core).wait_send()
        relay_a(z, 1, core).wait_send()
        cross_a(z, 1 - core).wait_send()
        across(z).wait_send()
        return carry

    line(across_z(zl), zl).wait_send()
    to_mate(zl, x_low).wait_send()
    to_mate(across_z(zl), x_low).wait_send()
    lax.fori_loop(1, n.zs, drain_line, 0)
    lax.fori_loop(1, n.group, drain_near, 0)
    lax.fori_loop(0, n.zs, drain_line_all, 0)

    def drain_plane(d, carry):
        j = other(d)
        share(j, spot).wait_send()
        to_plane(pl.ds(0, n.cols), j, spot).wait_send()
        return carry

    lax.fori_loop(1, n.spots, drain_plane, 0)

    def drain_plane_all(j, carry):
        relay_b(j, core).wait_send()
        return carry

    lax.fori_loop(0, n.spots, drain_plane_all, 0)
    for yy in range(n.ys):
        if yy not in ys_of(last):
            cross_b(yy, 1 - core).wait_send()
            continue
        for xx in range(n.xs):
            to_plane_over(pl.ds(0, n.cols), yy * n.xs + xx, spot).wait_send()

    back.wait_recv()
    out[...] = c_pad[:, 0 : n.rows] + fin_in[:, 0 : n.rows]
    back.wait_send()


def per_device(mesh, coefficients, integrals, targets, orbital_pairs, phases):
    rows, cols = coefficients.shape
    n = plan_of(
        mesh, (rows * mesh.shape["tile"], cols * mesh.shape["wide"]), targets.shape, integrals.shape[0]
    )
    bf16, f32 = jnp.bfloat16, jnp.float32
    total = n.own * LANES
    piece = (n.cols, LANES)
    dma, vmem = pltpu.SemaphoreType.DMA, pltpu.VMEM
    here, anywhere = pl.BlockSpec(memory_space=pltpu.VMEM), pl.BlockSpec(memory_space=pl.ANY)
    sigma_t = pl.pallas_call(
        functools.partial(kernel, n),
        out_shape=jax.ShapeDtypeStruct((n.cols, n.rows), f32),
        in_specs=[here, here, anywhere, anywhere, anywhere],
        out_specs=here,
        scratch_shapes=[
            vmem((3, n.exc, 2 * LANES), jnp.int32),
            vmem((3, LANES, 2 * LANES), jnp.int32),
            vmem((n.pair_pad, n.pair_pad), bf16),
            vmem((n.step * LANES, n.pair_pad), bf16),
            vmem(piece, f32),
            vmem(piece, bf16),
            vmem(piece, bf16),
            vmem((2, n.spots, *piece), bf16),
            vmem((2, 2, n.zs, *piece), bf16),
            vmem((n.strings, LANES), f32),
            vmem((2 * LANES, n.strings), bf16),
            vmem((total, n.strings), bf16),
            vmem((n.own, LANES, LANES), bf16),
            vmem((2 * LANES, total), bf16),
            vmem((2 * LANES, n.strings), f32),
            vmem((n.tiles, 2 * n.cols, LANES), f32),
            vmem((n.strings, LANES), bf16),
            vmem((n.strings, LANES), bf16),
            vmem((n.strings, LANES), bf16),
            vmem((n.tiles, 2 * n.cols, LANES), bf16),
            vmem((n.tiles, 2 * n.cols, LANES), bf16),
            vmem((n.zs, *piece), bf16),
            vmem((n.zs, *piece), bf16),
            vmem((n.zs, *piece), bf16),
            vmem((n.spots, *piece), bf16),
            vmem((n.spots, *piece), bf16),
            vmem((n.zs, *piece), bf16),
            vmem(piece, f32),
            vmem(piece, f32),
            dma((3,)),
            dma((1,)),
            dma((1,)),
            dma((n.spots,)),
            dma((n.spots,)),
            dma((n.spots,)),
            dma((n.spots,)),
            dma((n.zs,)),
            dma((n.zs,)),
            dma((n.zs,)),
            dma((n.zs,)),
            dma((n.zs,)),
            dma((n.zs,)),
            dma((2, n.zs)),
            dma((2, n.zs)),
            dma((n.ys,)),
            dma((n.ys,)),
            dma((n.zs,)),
            dma((n.zs,)),
            dma((n.spots,)),
            dma((n.spots,)),
            dma((n.spots,)),
            dma((n.spots,)),
            dma((n.zs,)),
            dma((n.zs,)),
            dma((n.zs,)),
            dma((n.zs,)),
            dma((1,)),
            dma((1,)),
        ],
        compiler_params=pltpu.CompilerParams(
            collective_id=0, has_side_effects=True, vmem_limit_bytes=56 * 1024 * 1024
        ),
        name="sigma",
    )(coefficients.T, integrals, targets, orbital_pairs, phases)
    return sigma_t.T


def solution(mesh):
    in_specs = (P("tile", "wide"), P(), P(), P(), P())
    return jax.shard_map(
        functools.partial(per_device, mesh),
        mesh=mesh,
        in_specs=in_specs,
        out_specs=P("tile", "wide"),
        check_vma=False,
    )
```

```python
import functools
import types

import jax
import jax.numpy as jnp
from jax import lax
from jax.experimental import pallas as pl
from jax.experimental.pallas import tpu as pltpu
from jax.sharding import PartitionSpec as P

LANES = 128
MESH = pl.DeviceIdType.MESH


def plan_of(mesh, coef_shape, exc_shape, pair_count):
    tiles, wides = mesh.shape["tile"], mesh.shape["wide"]
    xs = 4 if wides == 32 else 2
    ys = wides // (2 * xs)
    zs = tiles // 2
    strings = coef_shape[0]
    ranges = strings // (3 * LANES)
    return types.SimpleNamespace(
        tiles=tiles,
        xs=xs,
        ys=ys,
        zs=zs,
        far=99,
        spots=xs * ys,
        strings=strings,
        rows=strings // tiles,
        cols=strings // wides,
        own=strings // (xs * ys * 2),
        exc=exc_shape[0],
        pairs=pair_count,
        pair_pad=-(-pair_count // LANES) * LANES,
        step=8,
        ranges=ranges,
        order=sorted(range(ranges), key=lambda h: -abs(2 * h - ranges + 1)),
        width=strings // ranges,
    )


def kernel(n, coef, integ, tgt, prs, phs, out, raw, tabs, g_pad, p_part, c_pad, first, hold, gath_b, gath_a,
           xt, x_all, t_all, w_all, u_all, part, xa, sb, rb, ob, sa, ra, sx, rx, oa, in_b, in_c, in_a, fin, fin_in,
           s_tab, s1, r1, s2b, r2b, s5b, r5b, s2a, r2a, sxa, rxa, sxd, s5a, r5a, s6b, r6b, s6a, r6a,
           s3b, r3b, s3c, r3c, s7, r7, s8, r8, s4, r4):
    bf16, f32 = jnp.bfloat16, jnp.float32
    tile, wide = lax.axis_index("tile"), lax.axis_index("wide")
    core, zl = lax.rem(tile, 2), tile // 2
    x, zh, y = lax.rem(wide, n.xs), lax.rem(wide // n.xs, 2), wide // (2 * n.xs)
    spot = y * n.xs + x
    x_low, x_high = lax.rem(x, 2), x // 2

    def device(xx, yy, zzh, zzl, cc):
        return (zzl * 2 + cc, (yy * 2 + zzh) * n.xs + xx)

    def at_spot(j):
        return device(lax.rem(j, n.xs), j // n.xs, zh, zl, core)

    def on_line(z):
        return device(x, y, zh, z, core)

    def on_mates_line(z):
        return device(x_high * 2 + 1 - x_low, y, zh, z, core)

    def at_spot_over(j):
        return device(lax.rem(j, n.xs), j // n.xs, zh, zl, 1 - core)

    def is_far(z):
        return jnp.abs(z - zl) >= n.far

    def near_first(i):
        return jnp.where(zl < n.zs // 2, i, n.zs - 1 - i)

    def other(d):
        return lax.rem(spot + d, n.spots)

    def other_z(d):
        return lax.rem(zl + d, n.zs)

    partner = device(x, y, zh, zl, 1 - core)
    mate = device(x_high * 2 + 1 - x_low, y, zh, zl, core)
    half = n.zs // 2
    far_z = lax.rem(zl + half + n.zs * core, 2 * n.zs)
    far_out = device(x, y, far_z // n.zs, lax.rem(far_z, n.zs), zh)
    back_z = zh * n.zs + zl + 2 * n.zs - half
    back_zl = lax.rem(back_z, n.zs)
    far_in = device(x, y, core, back_zl, lax.rem(back_z - back_zl, 2 * n.zs) // n.zs)

    def remote(src, dst, send, recv, to):
        return pltpu.make_async_remote_copy(
            src_ref=src, dst_ref=dst, send_sem=send, recv_sem=recv, device_id=to, device_id_type=MESH
        )

    place = lax.rem(y * (n.xs // 2) + x_high + zl, n.zs)
    start = ((x_low * 2 + core) * n.zs + place) * n.own
    window = jnp.minimum(start // LANES * LANES, n.strings - 2 * LANES)
    window = pl.multiple_of(window, LANES)
    loads = [
        pltpu.make_async_copy(ref.at[:, pl.ds(window, 2 * LANES)], raw.at[i], s_tab.at[i])
        for i, ref in enumerate((tgt, prs, phs))
    ]
    for load in loads:
        load.start()

    barrier = pltpu.get_barrier_semaphore()

    def greet(whom):
        pl.semaphore_signal(barrier, inc=1, device_id=whom, device_id_type=MESH)

    def greet_line(d, carry):
        greet(on_line(other_z(d)))
        return carry

    def greet_plane(d, carry):
        greet(at_spot(other(d)))
        greet(at_spot_over(other(d)))
        return carry

    greet(far_out)
    greet(far_in)
    lax.fori_loop(1, n.zs, greet_line, 0)
    lax.fori_loop(1, n.spots, greet_plane, 0)
    greet(partner)

    c_pad[...] = jnp.zeros_like(c_pad)
    c_pad[:, 0 : n.rows] = coef[...].astype(f32)
    first[...] = c_pad[...].astype(bf16)

    g_pad[...] = jnp.zeros_like(g_pad)
    g_pad[0 : n.pairs, 0 : n.pairs] = integ[...]
    tabs[...] = jnp.zeros_like(tabs)
    for load in loads:
        load.wait()
    tabs[:, 0 : n.exc] = raw[...]

    offset = start - window
    lane = lax.broadcasted_iota(jnp.int32, (LANES, LANES), 1).astype(f32).astype(bf16)
    one, zero = jnp.ones((), bf16), jnp.zeros((), bf16)

    def spread_col(col):
        return jnp.broadcast_to(col, (LANES, LANES)).astype(bf16)

    def build(it, carry):
        shift = lax.rem(2 * 2 * LANES - offset - it * n.step, 2 * LANES)
        t = pltpu.roll(tabs[0], shift, 1)[:, 0:LANES]
        q = pltpu.roll(tabs[1], shift, 1)[:, 0:LANES]
        s = pltpu.roll(tabs[2], shift, 1)[:, 0:LANES].astype(f32)
        t_hi, t_lo = (t // LANES).astype(f32), lax.rem(t, LANES).astype(f32)
        q_hi, q_lo = (q // LANES).astype(f32), lax.rem(q, LANES).astype(f32)
        for u in range(n.step):
            hi, lo = spread_col(q_hi[:, u : u + 1]), spread_col(q_lo[:, u : u + 1])
            sign = spread_col(s[:, u : u + 1])
            hot = jnp.where(lo == lane, sign, zero)
            for kt in range(n.pair_pad // LANES):
                p_part[u * LANES : (u + 1) * LANES, kt * LANES : (kt + 1) * LANES] = jnp.where(
                    hi == kt, hot, zero
                )
        picked = lax.dot_general(
            p_part[...], g_pad[...], (((1,), (1,)), ((), ())), preferred_element_type=f32
        ).astype(bf16)
        for u in range(n.step):
            b = it * n.step + u
            rows = pl.ds(pl.multiple_of(b * LANES, LANES), LANES)
            hi, lo = spread_col(t_hi[:, u : u + 1]), spread_col(t_lo[:, u : u + 1])
            hot = jnp.where(lo == lane, one, zero)
            for kt in range(n.strings // LANES):
                t_all[rows, kt * LANES : (kt + 1) * LANES] = jnp.where(hi == kt, hot, zero)
        for u in range(n.step):
            rows = slice(u * LANES, (u + 1) * LANES)
            w_all[it * n.step + u] = lax.dot_general(
                picked[rows], p_part[rows], (((1,), (1,)), ((), ())), preferred_element_type=f32
            ).astype(bf16)
        return carry

    builds = n.own // n.step
    cuts = [2, 4, 6, 6, 6]

    lax.fori_loop(0, 2, build, 0)
    pl.semaphore_wait(barrier, 2 + (n.zs - 1) + 2 * (n.spots - 1) + 1)

    def line(to, frm):
        return remote(first, gath_a.at[core, x_low, frm], s2a.at[to], r2a.at[frm], on_line(to))

    def line_over(to):
        return remote(first, gath_a.at[core, x_low, zl], sxd.at[to], rxa.at[zl], on_mates_line(to))

    def to_mate(z, side):
        ref = gath_a.at[core, side, z]
        return remote(ref, ref, sxa.at[z], rxa.at[z], mate)

    def relay_a(z, side, cc):
        ref = gath_a.at[cc, side, z]
        return remote(ref, ref, s5a.at[side, z], r5a.at[side, z], partner)

    def share(to, frm):
        return remote(hold, gath_b.at[core, frm], s2b.at[to], r2b.at[frm], at_spot(to))

    def relay_b(j, cc):
        ref = gath_b.at[cc, j]
        return remote(ref, ref, s5b.at[j], r5b.at[j], partner)

    forth = remote(first, hold, s1.at[0], r1.at[0], far_out)
    forth.start()

    def start_line(d, carry):
        line(other_z(d), zl).start()
        return carry

    lax.fori_loop(1, n.zs, start_line, 0)
    gath_a[core, x_low, zl] = first[...]
    to_mate(zl, x_low).start()
    relay_a(zl, x_low, core).start()

    lax.fori_loop(cuts[0], cuts[1], build, 0)

    forth.wait_recv()

    def start_share(d, carry):
        share(other(d), spot).start()
        return carry

    lax.fori_loop(1, n.spots, start_share, 0)
    gath_b[core, spot] = hold[...]
    relay_b(spot, core).start()

    lax.fori_loop(cuts[1], cuts[2], build, 0)

    def hand_line(d, carry):
        z = other_z(d)
        line(zl, z).wait_recv()
        to_mate(z, x_low).start()
        relay_a(z, x_low, core).start()
        return carry

    lax.fori_loop(1, n.zs, hand_line, 0)

    def hand_plane(d, carry):
        j = other(d)
        share(spot, j).wait_recv()
        relay_b(j, core).start()
        return carry

    lax.fori_loop(1, n.spots, hand_plane, 0)

    def hand_mate(d, carry):
        z = other_z(d)
        to_mate(z, 1 - x_low).wait_recv()
        relay_a(z, 1 - x_low, core).start()
        return carry

    lax.fori_loop(0, n.zs, hand_mate, 0)
    lax.fori_loop(cuts[3], cuts[4], build, 0)

    def wait_relay_b(j, carry):
        relay_b(j, 1 - core).wait_recv()
        return carry

    lax.fori_loop(0, n.spots, wait_relay_b, 0)

    for w in range(2 * n.spots):
        yy, cc, xx = w // (2 * n.xs), w // n.xs % 2, w % n.xs
        xt[w * n.cols : (w + 1) * n.cols] = gath_b[cc, yy * n.xs + xx].astype(f32)
    for kt in range(n.strings // LANES):
        at = slice(kt * LANES, (kt + 1) * LANES)
        x_all[0:LANES, at] = xt[at].T.astype(bf16)

    def wait_relay_a(z, carry):
        relay_a(z, 0, 1 - core).wait_recv()
        relay_a(z, 1, 1 - core).wait_recv()
        return carry

    lax.fori_loop(0, n.zs, wait_relay_a, 0)

    lane_i = lax.broadcasted_iota(jnp.int32, (LANES, LANES), 1)
    spare = jnp.zeros((LANES - 2 * n.cols, LANES), f32)

    def alpha_piece(t):
        low, high = (gath_a[t % 2, side, t // 2].astype(f32) for side in range(2))
        return jnp.concatenate([low, high, spare], axis=0)

    for four in range(n.tiles // 4):
        p0, p1, p2, p3 = (alpha_piece(4 * four + i) for i in range(4))
        p1, p2, p3 = pltpu.roll(p1, 96, 1), pltpu.roll(p2, 64, 1), pltpu.roll(p3, 32, 1)
        tiles3 = (
            jnp.where(lane_i < 96, p0, p1),
            jnp.where(lane_i < 64, p1, p2),
            jnp.where(lane_i < 32, p2, p3),
        )
        for i, value in enumerate(tiles3):
            at = (3 * four + i) * LANES
            x_all[LANES : 2 * LANES, at : at + LANES] = value.astype(bf16)

    many = min(16, n.own)

    def couple(it, carry):
        rows = pl.ds(pl.multiple_of(it * many * LANES, many * LANES), many * LANES)
        v = lax.dot_general(
            x_all[...], t_all[rows, :], (((1,), (1,)), ((), ())), preferred_element_type=f32
        ).astype(bf16)
        for u in range(many):
            value = jnp.dot(
                v[:, u * LANES : (u + 1) * LANES], w_all[it * many + u], preferred_element_type=f32
            )
            at = pl.ds(pl.multiple_of((it * many + u) * LANES, LANES), LANES)
            u_all[:, at] = value.astype(bf16)
        return carry

    lax.fori_loop(0, n.own // many, couple, 0)

    block = n.xs * n.cols
    keep = pl.ds(pl.multiple_of(x_low * n.cols, 16), n.cols)
    pass_on = pl.ds(pl.multiple_of((1 - x_low) * n.cols, 16), n.cols)

    def block_rows(yy, cc):
        return pl.ds(pl.multiple_of((yy * 2 + cc) * block, 16), block)

    def ys_of(h):
        return range(h * n.ys // n.ranges, (h + 1) * n.ys // n.ranges)

    def zs_of(h):
        return range(h * n.zs // n.ranges, (h + 1) * n.zs // n.ranges)

    def cross_b(yy, cc):
        rows = block_rows(yy, cc)
        return remote(sb.at[rows], rb.at[rows], s6b.at[yy], r6b.at[yy], partner)

    def cross_a(z, cc):
        return remote(sa.at[2 * z + cc], ra.at[2 * z + cc], s6a.at[z], r6a.at[z], partner)

    def across(z):
        return remote(sx.at[z], rx.at[z], s7.at[z], r7.at[z], mate)

    def down_line(to, frm):
        return remote(oa.at[to], in_a.at[frm], s8.at[to], r8.at[frm], on_line(to))

    def to_plane(rows, to, frm):
        return remote(ob.at[rows], in_b.at[frm], s3b.at[to], r3b.at[frm], at_spot(to))

    def to_plane_over(rows, to, frm):
        return remote(ob.at[rows], in_c.at[frm], s3c.at[to], r3c.at[frm], at_spot_over(to))

    def piece_rows(yy, cc, xx):
        return pl.ds(pl.multiple_of(((yy * 2 + cc) * n.xs + xx) * n.cols, 16), n.cols)

    last = n.order[-1]

    def scatter(h):
        at = slice(h * n.width, (h + 1) * n.width)
        part[:, at] = jnp.dot(u_all[...], t_all[:, at], preferred_element_type=f32)

    def sum_cores(h):
        t0, t1, t2 = (
            part[LANES : 2 * LANES, (3 * h + i) * LANES : (3 * h + i + 1) * LANES] for i in range(3)
        )
        roll = functools.partial(pltpu.roll, axis=1)
        values = (
            t0,
            jnp.where(lane_i < 32, roll(t0, 32), roll(t1, 32)),
            jnp.where(lane_i < 64, roll(t1, 64), roll(t2, 64)),
            roll(t2, 96),
        )
        for i, value in enumerate(values):
            xa[4 * h + i] = value[0 : 2 * n.cols]
        for z in zs_of(h):
            sa[2 * z + 1 - core] = xa[2 * z + 1 - core].astype(bf16)
            cross_a(z, 1 - core).start()
        for kt in range(3 * h, 3 * h + 3):
            at = slice(kt * LANES, (kt + 1) * LANES)
            xt[at] = part[0:LANES, at].T
        for yy in ys_of(h):
            if h == last:
                rows = pl.ds(yy * 2 * block, 2 * block)
                ob[rows] = xt[rows].astype(bf16)
                for i in range(n.xs):
                    xx = lax.rem(x + i, n.xs)
                    to_plane_over(piece_rows(yy, 1 - core, xx), yy * n.xs + xx, spot).start()

                    @pl.when(jnp.logical_or(xx != x, y != yy))
                    def _():
                        to_plane(piece_rows(yy, core, xx), yy * n.xs + xx, spot).start()

            else:
                rows = block_rows(yy, 1 - core)
                sb[rows] = xt[rows].astype(bf16)
                cross_b(yy, 1 - core).start()

    def sum_mates(h):
        for z in zs_of(h):
            cross_a(z, core).wait_recv()
            xa[2 * z + core] = xa[2 * z + core] + ra[2 * z + core].astype(f32)
            sx[z] = xa[2 * z + core, pass_on].astype(bf16)
            across(z).start()
        for yy in ys_of(h) if h != last else ():
            rows = block_rows(yy, core)
            cross_b(yy, core).wait_recv()
            total = xt[rows] + rb[rows].astype(f32)
            xt[rows] = total
            ob[rows] = total.astype(bf16)
            for i in range(n.xs):
                xx = lax.rem(x + i, n.xs)

                @pl.when(jnp.logical_or(xx != x, y != yy))
                def _():
                    to_plane(piece_rows(yy, core, xx), yy * n.xs + xx, spot).start()

    def sum_line(h):
        for z in zs_of(h):
            across(z).wait_recv()
            total = xa[2 * z + core, keep] + rx[z].astype(f32)
            xa[2 * z + core, keep] = total
            oa[z] = total.astype(bf16)

            @pl.when(z != zl)
            def _():
                down_line(z, zl).start()

    for i in range(n.ranges + 2):
        if i < n.ranges:
            scatter(n.order[i])
        if 0 <= i - 2 < n.ranges:
            sum_line(n.order[i - 2])
        if 0 <= i - 1 < n.ranges:
            sum_mates(n.order[i - 1])
        if i < n.ranges:
            sum_cores(n.order[i])

    in_b[spot] = jnp.zeros_like(first)

    def wait_plane(d, carry):
        to_plane(pl.ds(0, n.cols), spot, other(d)).wait_recv()
        return carry

    def wait_over(j, carry):
        to_plane_over(pl.ds(0, n.cols), spot, j).wait_recv()
        return carry

    def total_of(ref, count):
        terms = [ref[j].astype(f32) for j in range(count)]
        while len(terms) > 1:
            terms = [a + b for a, b in zip(terms[::2], terms[1::2])] + terms[len(terms) & ~1 :]
        return terms[0]

    in_last = (y >= ys_of(last)[0]) & (y <= ys_of(last)[-1])
    lax.fori_loop(1, n.spots, wait_plane, 0)
    fin[...] = xt[piece_rows(y, core, x)] + total_of(in_b, n.spots)

    @pl.when(in_last)
    def _():
        lax.fori_loop(0, n.spots, wait_over, 0)
        fin[...] += total_of(in_c, n.spots)

    back = remote(fin, fin_in, s4.at[0], r4.at[0], far_in)
    back.start()

    in_a[zl] = jnp.zeros_like(first)

    def wait_line(d, carry):
        down_line(zl, other_z(d)).wait_recv()
        return carry

    lax.fori_loop(1, n.zs, wait_line, 0)
    c_pad[...] = xa[2 * zl + core, keep] + total_of(in_a, n.zs)

    forth.wait_send()

    def drain_line(d, carry):
        z = other_z(d)
        line(z, zl).wait_send()
        down_line(z, zl).wait_send()

        @pl.when(is_far(z))
        def _():
            line_over(z).wait_send()

        return carry

    lax.fori_loop(1, n.zs, drain_line, 0)

    def drain_line_all(z, carry):
        @pl.when(jnp.logical_not(is_far(z)))
        def _():
            to_mate(z, x_low).wait_send()

        relay_a(z, 0, core).wait_send()
        relay_a(z, 1, core).wait_send()
        cross_a(z, 1 - core).wait_send()
        across(z).wait_send()
        return carry

    lax.fori_loop(0, n.zs, drain_line_all, 0)

    def drain_plane(d, carry):
        j = other(d)
        share(j, spot).wait_send()
        to_plane(pl.ds(0, n.cols), j, spot).wait_send()
        return carry

    lax.fori_loop(1, n.spots, drain_plane, 0)

    def drain_plane_all(j, carry):
        relay_b(j, core).wait_send()
        return carry

    lax.fori_loop(0, n.spots, drain_plane_all, 0)
    for yy in range(n.ys):
        if yy not in ys_of(last):
            cross_b(yy, 1 - core).wait_send()
            continue
        for xx in range(n.xs):
            to_plane_over(pl.ds(0, n.cols), yy * n.xs + xx, spot).wait_send()

    back.wait_recv()
    out[...] = c_pad[:, 0 : n.rows] + fin_in[:, 0 : n.rows]
    back.wait_send()


def per_device(mesh, coefficients, integrals, targets, orbital_pairs, phases):
    rows, cols = coefficients.shape
    n = plan_of(
        mesh, (rows * mesh.shape["tile"], cols * mesh.shape["wide"]), targets.shape, integrals.shape[0]
    )
    bf16, f32 = jnp.bfloat16, jnp.float32
    total = n.own * LANES
    piece = (n.cols, LANES)
    dma, vmem = pltpu.SemaphoreType.DMA, pltpu.VMEM
    here, anywhere = pl.BlockSpec(memory_space=pltpu.VMEM), pl.BlockSpec(memory_space=pl.ANY)
    sigma_t = pl.pallas_call(
        functools.partial(kernel, n),
        out_shape=jax.ShapeDtypeStruct((n.cols, n.rows), f32),
        in_specs=[here, here, anywhere, anywhere, anywhere],
        out_specs=here,
        scratch_shapes=[
            vmem((3, n.exc, 2 * LANES), jnp.int32),
            vmem((3, LANES, 2 * LANES), jnp.int32),
            vmem((n.pair_pad, n.pair_pad), bf16),
            vmem((n.step * LANES, n.pair_pad), bf16),
            vmem(piece, f32),
            vmem(piece, bf16),
            vmem(piece, bf16),
            vmem((2, n.spots, *piece), bf16),
            vmem((2, 2, n.zs, *piece), bf16),
            vmem((n.strings, LANES), f32),
            vmem((2 * LANES, n.strings), bf16),
            vmem((total, n.strings), bf16),
            vmem((n.own, LANES, LANES), bf16),
            vmem((2 * LANES, total), bf16),
            vmem((2 * LANES, n.strings), f32),
            vmem((n.tiles, 2 * n.cols, LANES), f32),
            vmem((n.strings, LANES), bf16),
            vmem((n.strings, LANES), bf16),
            vmem((n.strings, LANES), bf16),
            vmem((n.tiles, 2 * n.cols, LANES), bf16),
            vmem((n.tiles, 2 * n.cols, LANES), bf16),
            vmem((n.zs, *piece), bf16),
            vmem((n.zs, *piece), bf16),
            vmem((n.zs, *piece), bf16),
            vmem((n.spots, *piece), bf16),
            vmem((n.spots, *piece), bf16),
            vmem((n.zs, *piece), bf16),
            vmem(piece, f32),
            vmem(piece, f32),
            dma((3,)),
            dma((1,)),
            dma((1,)),
            dma((n.spots,)),
            dma((n.spots,)),
            dma((n.spots,)),
            dma((n.spots,)),
            dma((n.zs,)),
            dma((n.zs,)),
            dma((n.zs,)),
            dma((n.zs,)),
            dma((n.zs,)),
            dma((2, n.zs)),
            dma((2, n.zs)),
            dma((n.ys,)),
            dma((n.ys,)),
            dma((n.zs,)),
            dma((n.zs,)),
            dma((n.spots,)),
            dma((n.spots,)),
            dma((n.spots,)),
            dma((n.spots,)),
            dma((n.zs,)),
            dma((n.zs,)),
            dma((n.zs,)),
            dma((n.zs,)),
            dma((1,)),
            dma((1,)),
        ],
        compiler_params=pltpu.CompilerParams(
            collective_id=0, has_side_effects=True, vmem_limit_bytes=56 * 1024 * 1024
        ),
        name="sigma",
    )(coefficients.T, integrals, targets, orbital_pairs, phases)
    return sigma_t.T


def solution(mesh):
    in_specs = (P("tile", "wide"), P(), P(), P(), P())
    return jax.shard_map(
        functools.partial(per_device, mesh),
        mesh=mesh,
        in_specs=in_specs,
        out_specs=P("tile", "wide"),
        check_vma=False,
    )
```

```python
import functools
import types

import jax
import jax.numpy as jnp
from jax import lax
from jax.experimental import pallas as pl
from jax.experimental.pallas import tpu as pltpu
from jax.sharding import PartitionSpec as P

LANES = 128
MESH = pl.DeviceIdType.MESH


def plan_of(mesh, coef_shape, exc_shape, pair_count):
    tiles, wides = mesh.shape["tile"], mesh.shape["wide"]
    xs = 4 if wides == 32 else 2
    ys = wides // (2 * xs)
    zs = tiles // 2
    strings = coef_shape[0]
    ranges = strings // (3 * LANES)
    return types.SimpleNamespace(
        tiles=tiles,
        xs=xs,
        ys=ys,
        zs=zs,
        far=99,
        spots=xs * ys,
        strings=strings,
        rows=strings // tiles,
        cols=strings // wides,
        own=strings // (xs * ys * 2),
        exc=exc_shape[0],
        pairs=pair_count,
        pair_pad=-(-pair_count // LANES) * LANES,
        step=8,
        ranges=ranges,
        groups=((0, 1), (3,), (2,)) if ranges == 4 else tuple((h,) for h in range(ranges)),
        width=strings // ranges,
    )


def kernel(n, coef, integ, tgt, prs, phs, out, raw, tabs, g_pad, p_part, c_pad, first, hold, gath_b, gath_a,
           xt, x_all, t_all, w_all, u_all, part, xa, sb, rb, ob, sa, ra, sx, rx, oa, in_b, in_c, in_a, fin, fin_in,
           s_tab, s1, r1, s2b, r2b, s5b, r5b, s2a, r2a, sxa, rxa, sxd, s5a, r5a, s6b, r6b, s6a, r6a,
           s3b, r3b, s3c, r3c, s7, r7, s8, r8, s4, r4):
    bf16, f32 = jnp.bfloat16, jnp.float32
    tile, wide = lax.axis_index("tile"), lax.axis_index("wide")
    core, zl = lax.rem(tile, 2), tile // 2
    x, zh, y = lax.rem(wide, n.xs), lax.rem(wide // n.xs, 2), wide // (2 * n.xs)
    spot = y * n.xs + x
    x_low, x_high = lax.rem(x, 2), x // 2

    def device(xx, yy, zzh, zzl, cc):
        return (zzl * 2 + cc, (yy * 2 + zzh) * n.xs + xx)

    def at_spot(j):
        return device(lax.rem(j, n.xs), j // n.xs, zh, zl, core)

    def on_line(z):
        return device(x, y, zh, z, core)

    def on_mates_line(z):
        return device(x_high * 2 + 1 - x_low, y, zh, z, core)

    def at_spot_over(j):
        return device(lax.rem(j, n.xs), j // n.xs, zh, zl, 1 - core)

    def is_far(z):
        return jnp.abs(z - zl) >= n.far

    def near_first(i):
        return jnp.where(zl < n.zs // 2, i, n.zs - 1 - i)

    def other(d):
        return lax.rem(spot + d, n.spots)

    def other_z(d):
        return lax.rem(zl + d, n.zs)

    partner = device(x, y, zh, zl, 1 - core)
    mate = device(x_high * 2 + 1 - x_low, y, zh, zl, core)
    half = n.zs // 2
    far_z = lax.rem(zl + half + n.zs * core, 2 * n.zs)
    far_out = device(x, y, far_z // n.zs, lax.rem(far_z, n.zs), zh)
    back_z = zh * n.zs + zl + 2 * n.zs - half
    back_zl = lax.rem(back_z, n.zs)
    far_in = device(x, y, core, back_zl, lax.rem(back_z - back_zl, 2 * n.zs) // n.zs)

    def remote(src, dst, send, recv, to):
        return pltpu.make_async_remote_copy(
            src_ref=src, dst_ref=dst, send_sem=send, recv_sem=recv, device_id=to, device_id_type=MESH
        )

    place = lax.rem(y * (n.xs // 2) + x_high + zl, n.zs)
    start = ((x_low * 2 + core) * n.zs + place) * n.own
    window = jnp.minimum(start // LANES * LANES, n.strings - 2 * LANES)
    window = pl.multiple_of(window, LANES)
    loads = [
        pltpu.make_async_copy(ref.at[:, pl.ds(window, 2 * LANES)], raw.at[i], s_tab.at[i])
        for i, ref in enumerate((tgt, prs, phs))
    ]
    for load in loads:
        load.start()

    barrier = pltpu.get_barrier_semaphore()

    def greet(whom):
        pl.semaphore_signal(barrier, inc=1, device_id=whom, device_id_type=MESH)

    def greet_line(d, carry):
        greet(on_line(other_z(d)))
        return carry

    def greet_plane(d, carry):
        greet(at_spot(other(d)))
        greet(at_spot_over(other(d)))
        return carry

    greet(far_out)
    greet(far_in)
    lax.fori_loop(1, n.zs, greet_line, 0)
    lax.fori_loop(1, n.spots, greet_plane, 0)
    greet(partner)

    c_pad[...] = jnp.zeros_like(c_pad)
    c_pad[:, 0 : n.rows] = coef[...].astype(f32)
    first[...] = c_pad[...].astype(bf16)

    g_pad[...] = jnp.zeros_like(g_pad)
    g_pad[0 : n.pairs, 0 : n.pairs] = integ[...]
    tabs[...] = jnp.zeros_like(tabs)
    for load in loads:
        load.wait()
    tabs[:, 0 : n.exc] = raw[...]

    offset = start - window
    lane = lax.broadcasted_iota(jnp.int32, (LANES, LANES), 1).astype(f32).astype(bf16)
    one, zero = jnp.ones((), bf16), jnp.zeros((), bf16)

    def spread_col(col):
        return jnp.broadcast_to(col, (LANES, LANES)).astype(bf16)

    def build(it, carry):
        shift = lax.rem(2 * 2 * LANES - offset - it * n.step, 2 * LANES)
        t = pltpu.roll(tabs[0], shift, 1)[:, 0:LANES]
        q = pltpu.roll(tabs[1], shift, 1)[:, 0:LANES]
        s = pltpu.roll(tabs[2], shift, 1)[:, 0:LANES].astype(f32)
        t_hi, t_lo = (t // LANES).astype(f32), lax.rem(t, LANES).astype(f32)
        q_hi, q_lo = (q // LANES).astype(f32), lax.rem(q, LANES).astype(f32)
        for u in range(n.step):
            hi, lo = spread_col(q_hi[:, u : u + 1]), spread_col(q_lo[:, u : u + 1])
            sign = spread_col(s[:, u : u + 1])
            hot = jnp.where(lo == lane, sign, zero)
            for kt in range(n.pair_pad // LANES):
                p_part[u * LANES : (u + 1) * LANES, kt * LANES : (kt + 1) * LANES] = jnp.where(
                    hi == kt, hot, zero
                )
        picked = lax.dot_general(
            p_part[...], g_pad[...], (((1,), (1,)), ((), ())), preferred_element_type=f32
        ).astype(bf16)
        for u in range(n.step):
            b = it * n.step + u
            rows = pl.ds(pl.multiple_of(b * LANES, LANES), LANES)
            hi, lo = spread_col(t_hi[:, u : u + 1]), spread_col(t_lo[:, u : u + 1])
            hot = jnp.where(lo == lane, one, zero)
            for kt in range(n.strings // LANES):
                t_all[rows, kt * LANES : (kt + 1) * LANES] = jnp.where(hi == kt, hot, zero)
        for u in range(n.step):
            rows = slice(u * LANES, (u + 1) * LANES)
            w_all[it * n.step + u] = lax.dot_general(
                picked[rows], p_part[rows], (((1,), (1,)), ((), ())), preferred_element_type=f32
            ).astype(bf16)
        return carry

    builds = n.own // n.step
    cuts = [2, 4, 6, 6, 6]

    lax.fori_loop(0, 2, build, 0)
    pl.semaphore_wait(barrier, 2 + (n.zs - 1) + 2 * (n.spots - 1) + 1)

    def line(to, frm):
        return remote(first, gath_a.at[core, x_low, frm], s2a.at[to], r2a.at[frm], on_line(to))

    def line_over(to):
        return remote(first, gath_a.at[core, x_low, zl], sxd.at[to], rxa.at[zl], on_mates_line(to))

    def to_mate(z, side):
        ref = gath_a.at[core, side, z]
        return remote(ref, ref, sxa.at[z], rxa.at[z], mate)

    def relay_a(z, side, cc):
        ref = gath_a.at[cc, side, z]
        return remote(ref, ref, s5a.at[side, z], r5a.at[side, z], partner)

    def share(to, frm):
        return remote(hold, gath_b.at[core, frm], s2b.at[to], r2b.at[frm], at_spot(to))

    def relay_b(j, cc):
        ref = gath_b.at[cc, j]
        return remote(ref, ref, s5b.at[j], r5b.at[j], partner)

    forth = remote(first, hold, s1.at[0], r1.at[0], far_out)
    forth.start()

    def start_line(d, carry):
        line(other_z(d), zl).start()
        return carry

    lax.fori_loop(1, n.zs, start_line, 0)
    gath_a[core, x_low, zl] = first[...]
    to_mate(zl, x_low).start()
    relay_a(zl, x_low, core).start()

    lax.fori_loop(cuts[0], cuts[1], build, 0)

    forth.wait_recv()

    def start_share(d, carry):
        share(other(d), spot).start()
        return carry

    lax.fori_loop(1, n.spots, start_share, 0)
    gath_b[core, spot] = hold[...]
    relay_b(spot, core).start()

    lax.fori_loop(cuts[1], cuts[2], build, 0)

    def hand_line(d, carry):
        z = other_z(d)
        line(zl, z).wait_recv()
        to_mate(z, x_low).start()
        relay_a(z, x_low, core).start()
        return carry

    lax.fori_loop(1, n.zs, hand_line, 0)

    def hand_plane(d, carry):
        j = other(d)
        share(spot, j).wait_recv()
        relay_b(j, core).start()
        return carry

    lax.fori_loop(1, n.spots, hand_plane, 0)

    def hand_mate(d, carry):
        z = other_z(d)
        to_mate(z, 1 - x_low).wait_recv()
        relay_a(z, 1 - x_low, core).start()
        return carry

    lax.fori_loop(0, n.zs, hand_mate, 0)
    lax.fori_loop(cuts[3], cuts[4], build, 0)

    def wait_relay_b(j, carry):
        relay_b(j, 1 - core).wait_recv()
        return carry

    lax.fori_loop(0, n.spots, wait_relay_b, 0)

    for w in range(2 * n.spots):
        yy, cc, xx = w // (2 * n.xs), w // n.xs % 2, w % n.xs
        xt[w * n.cols : (w + 1) * n.cols] = gath_b[cc, yy * n.xs + xx].astype(f32)
    for kt in range(n.strings // LANES):
        at = slice(kt * LANES, (kt + 1) * LANES)
        x_all[0:LANES, at] = xt[at].T.astype(bf16)

    def wait_relay_a(z, carry):
        relay_a(z, 0, 1 - core).wait_recv()
        relay_a(z, 1, 1 - core).wait_recv()
        return carry

    lax.fori_loop(0, n.zs, wait_relay_a, 0)

    lane_i = lax.broadcasted_iota(jnp.int32, (LANES, LANES), 1)
    spare = jnp.zeros((LANES - 2 * n.cols, LANES), f32)

    def alpha_piece(t):
        low, high = (gath_a[t % 2, side, t // 2].astype(f32) for side in range(2))
        return jnp.concatenate([low, high, spare], axis=0)

    for four in range(n.tiles // 4):
        p0, p1, p2, p3 = (alpha_piece(4 * four + i) for i in range(4))
        p1, p2, p3 = pltpu.roll(p1, 96, 1), pltpu.roll(p2, 64, 1), pltpu.roll(p3, 32, 1)
        tiles3 = (
            jnp.where(lane_i < 96, p0, p1),
            jnp.where(lane_i < 64, p1, p2),
            jnp.where(lane_i < 32, p2, p3),
        )
        for i, value in enumerate(tiles3):
            at = (3 * four + i) * LANES
            x_all[LANES : 2 * LANES, at : at + LANES] = value.astype(bf16)

    many = min(24, n.own)

    def couple(it, carry):
        rows = pl.ds(pl.multiple_of(it * many * LANES, many * LANES), many * LANES)
        v = lax.dot_general(
            x_all[...], t_all[rows, :], (((1,), (1,)), ((), ())), preferred_element_type=f32
        ).astype(bf16)
        for u in range(many):
            value = jnp.dot(
                v[:, u * LANES : (u + 1) * LANES], w_all[it * many + u], preferred_element_type=f32
            )
            at = pl.ds(pl.multiple_of((it * many + u) * LANES, LANES), LANES)
            u_all[:, at] = value.astype(bf16)
        return carry

    lax.fori_loop(0, n.own // many, couple, 0)

    block = n.xs * n.cols
    keep = pl.ds(pl.multiple_of(x_low * n.cols, 16), n.cols)
    pass_on = pl.ds(pl.multiple_of((1 - x_low) * n.cols, 16), n.cols)

    def block_rows(yy, cc):
        return pl.ds(pl.multiple_of((yy * 2 + cc) * block, 16), block)

    def ys_of(h):
        return range(h * n.ys // n.ranges, (h + 1) * n.ys // n.ranges)

    def zs_of(h):
        return range(h * n.zs // n.ranges, (h + 1) * n.zs // n.ranges)

    def cross_b(yy, cc):
        rows = block_rows(yy, cc)
        return remote(sb.at[rows], rb.at[rows], s6b.at[yy], r6b.at[yy], partner)

    def cross_a(z, cc):
        return remote(sa.at[2 * z + cc], ra.at[2 * z + cc], s6a.at[z], r6a.at[z], partner)

    def across(z):
        return remote(sx.at[z], rx.at[z], s7.at[z], r7.at[z], mate)

    def down_line(to, frm):
        return remote(oa.at[to], in_a.at[frm], s8.at[to], r8.at[frm], on_line(to))

    def to_plane(rows, to, frm):
        return remote(ob.at[rows], in_b.at[frm], s3b.at[to], r3b.at[frm], at_spot(to))

    def to_plane_over(rows, to, frm):
        return remote(ob.at[rows], in_c.at[frm], s3c.at[to], r3c.at[frm], at_spot_over(to))

    def piece_rows(yy, cc, xx):
        return pl.ds(pl.multiple_of(((yy * 2 + cc) * n.xs + xx) * n.cols, 16), n.cols)

    last = n.groups[-1][-1]

    def scatter(group):
        at = slice(group[0] * n.width, (group[-1] + 1) * n.width)
        part[:, at] = jnp.dot(u_all[...], t_all[:, at], preferred_element_type=f32)

    def sum_cores(h):
        t0, t1, t2 = (
            part[LANES : 2 * LANES, (3 * h + i) * LANES : (3 * h + i + 1) * LANES] for i in range(3)
        )
        roll = functools.partial(pltpu.roll, axis=1)
        values = (
            t0,
            jnp.where(lane_i < 32, roll(t0, 32), roll(t1, 32)),
            jnp.where(lane_i < 64, roll(t1, 64), roll(t2, 64)),
            roll(t2, 96),
        )
        for i, value in enumerate(values):
            xa[4 * h + i] = value[0 : 2 * n.cols]
        for z in zs_of(h):
            sa[2 * z + 1 - core] = xa[2 * z + 1 - core].astype(bf16)
            cross_a(z, 1 - core).start()
        for kt in range(3 * h, 3 * h + 3):
            at = slice(kt * LANES, (kt + 1) * LANES)
            xt[at] = part[0:LANES, at].T
        for yy in ys_of(h):
            if h == last:
                rows = pl.ds(yy * 2 * block, 2 * block)
                ob[rows] = xt[rows].astype(bf16)
                for i in range(n.xs):
                    xx = lax.rem(x + i, n.xs)
                    to_plane_over(piece_rows(yy, 1 - core, xx), yy * n.xs + xx, spot).start()

                    @pl.when(jnp.logical_or(xx != x, y != yy))
                    def _():
                        to_plane(piece_rows(yy, core, xx), yy * n.xs + xx, spot).start()

            else:
                rows = block_rows(yy, 1 - core)
                sb[rows] = xt[rows].astype(bf16)
                cross_b(yy, 1 - core).start()

    def sum_mates(h):
        for z in zs_of(h):
            cross_a(z, core).wait_recv()
            xa[2 * z + core] = xa[2 * z + core] + ra[2 * z + core].astype(f32)
            sx[z] = xa[2 * z + core, pass_on].astype(bf16)
            across(z).start()
        for yy in ys_of(h) if h != last else ():
            rows = block_rows(yy, core)
            cross_b(yy, core).wait_recv()
            total = xt[rows] + rb[rows].astype(f32)
            xt[rows] = total
            ob[rows] = total.astype(bf16)
            for i in range(n.xs):
                xx = lax.rem(x + i, n.xs)

                @pl.when(jnp.logical_or(xx != x, y != yy))
                def _():
                    to_plane(piece_rows(yy, core, xx), yy * n.xs + xx, spot).start()

    def sum_line(h):
        for z in zs_of(h):
            across(z).wait_recv()
            total = xa[2 * z + core, keep] + rx[z].astype(f32)
            xa[2 * z + core, keep] = total
            oa[z] = total.astype(bf16)

            @pl.when(z != zl)
            def _():
                down_line(z, zl).start()

    count = len(n.groups)
    for i in range(count + 2):
        if i < count:
            scatter(n.groups[i])
        for h in n.groups[i - 2] if 0 <= i - 2 < count else ():
            sum_line(h)
        for h in n.groups[i - 1] if 0 <= i - 1 < count else ():
            sum_mates(h)
        for h in n.groups[i] if i < count else ():
            sum_cores(h)

    in_b[spot] = jnp.zeros_like(first)

    def wait_plane(d, carry):
        to_plane(pl.ds(0, n.cols), spot, other(d)).wait_recv()
        return carry

    def wait_over(j, carry):
        to_plane_over(pl.ds(0, n.cols), spot, j).wait_recv()
        return carry

    def total_of(ref, count):
        terms = [ref[j].astype(f32) for j in range(count)]
        while len(terms) > 1:
            terms = [a + b for a, b in zip(terms[::2], terms[1::2])] + terms[len(terms) & ~1 :]
        return terms[0]

    in_last = (y >= ys_of(last)[0]) & (y <= ys_of(last)[-1])
    lax.fori_loop(1, n.spots, wait_plane, 0)
    fin[...] = xt[piece_rows(y, core, x)] + total_of(in_b, n.spots)

    @pl.when(in_last)
    def _():
        lax.fori_loop(0, n.spots, wait_over, 0)
        fin[...] += total_of(in_c, n.spots)

    back = remote(fin, fin_in, s4.at[0], r4.at[0], far_in)
    back.start()

    in_a[zl] = jnp.zeros_like(first)

    def wait_line(d, carry):
        down_line(zl, other_z(d)).wait_recv()
        return carry

    lax.fori_loop(1, n.zs, wait_line, 0)
    c_pad[...] = xa[2 * zl + core, keep] + total_of(in_a, n.zs)

    forth.wait_send()

    def drain_line(d, carry):
        z = other_z(d)
        line(z, zl).wait_send()
        down_line(z, zl).wait_send()

        @pl.when(is_far(z))
        def _():
            line_over(z).wait_send()

        return carry

    lax.fori_loop(1, n.zs, drain_line, 0)

    def drain_line_all(z, carry):
        @pl.when(jnp.logical_not(is_far(z)))
        def _():
            to_mate(z, x_low).wait_send()

        relay_a(z, 0, core).wait_send()
        relay_a(z, 1, core).wait_send()
        cross_a(z, 1 - core).wait_send()
        across(z).wait_send()
        return carry

    lax.fori_loop(0, n.zs, drain_line_all, 0)

    def drain_plane(d, carry):
        j = other(d)
        share(j, spot).wait_send()
        to_plane(pl.ds(0, n.cols), j, spot).wait_send()
        return carry

    lax.fori_loop(1, n.spots, drain_plane, 0)

    def drain_plane_all(j, carry):
        relay_b(j, core).wait_send()
        return carry

    lax.fori_loop(0, n.spots, drain_plane_all, 0)
    for yy in range(n.ys):
        if yy not in ys_of(last):
            cross_b(yy, 1 - core).wait_send()
            continue
        for xx in range(n.xs):
            to_plane_over(pl.ds(0, n.cols), yy * n.xs + xx, spot).wait_send()

    back.wait_recv()
    out[...] = c_pad[:, 0 : n.rows] + fin_in[:, 0 : n.rows]
    back.wait_send()


def per_device(mesh, coefficients, integrals, targets, orbital_pairs, phases):
    rows, cols = coefficients.shape
    n = plan_of(
        mesh, (rows * mesh.shape["tile"], cols * mesh.shape["wide"]), targets.shape, integrals.shape[0]
    )
    bf16, f32 = jnp.bfloat16, jnp.float32
    total = n.own * LANES
    piece = (n.cols, LANES)
    dma, vmem = pltpu.SemaphoreType.DMA, pltpu.VMEM
    here, anywhere = pl.BlockSpec(memory_space=pltpu.VMEM), pl.BlockSpec(memory_space=pl.ANY)
    sigma_t = pl.pallas_call(
        functools.partial(kernel, n),
        out_shape=jax.ShapeDtypeStruct((n.cols, n.rows), f32),
        in_specs=[here, here, anywhere, anywhere, anywhere],
        out_specs=here,
        scratch_shapes=[
            vmem((3, n.exc, 2 * LANES), jnp.int32),
            vmem((3, LANES, 2 * LANES), jnp.int32),
            vmem((n.pair_pad, n.pair_pad), bf16),
            vmem((n.step * LANES, n.pair_pad), bf16),
            vmem(piece, f32),
            vmem(piece, bf16),
            vmem(piece, bf16),
            vmem((2, n.spots, *piece), bf16),
            vmem((2, 2, n.zs, *piece), bf16),
            vmem((n.strings, LANES), f32),
            vmem((2 * LANES, n.strings), bf16),
            vmem((total, n.strings), bf16),
            vmem((n.own, LANES, LANES), bf16),
            vmem((2 * LANES, total), bf16),
            vmem((2 * LANES, n.strings), f32),
            vmem((n.tiles, 2 * n.cols, LANES), f32),
            vmem((n.strings, LANES), bf16),
            vmem((n.strings, LANES), bf16),
            vmem((n.strings, LANES), bf16),
            vmem((n.tiles, 2 * n.cols, LANES), bf16),
            vmem((n.tiles, 2 * n.cols, LANES), bf16),
            vmem((n.zs, *piece), bf16),
            vmem((n.zs, *piece), bf16),
            vmem((n.zs, *piece), bf16),
            vmem((n.spots, *piece), bf16),
            vmem((n.spots, *piece), bf16),
            vmem((n.zs, *piece), bf16),
            vmem(piece, f32),
            vmem(piece, f32),
            dma((3,)),
            dma((1,)),
            dma((1,)),
            dma((n.spots,)),
            dma((n.spots,)),
            dma((n.spots,)),
            dma((n.spots,)),
            dma((n.zs,)),
            dma((n.zs,)),
            dma((n.zs,)),
            dma((n.zs,)),
            dma((n.zs,)),
            dma((2, n.zs)),
            dma((2, n.zs)),
            dma((n.ys,)),
            dma((n.ys,)),
            dma((n.zs,)),
            dma((n.zs,)),
            dma((n.spots,)),
            dma((n.spots,)),
            dma((n.spots,)),
            dma((n.spots,)),
            dma((n.zs,)),
            dma((n.zs,)),
            dma((n.zs,)),
            dma((n.zs,)),
            dma((1,)),
            dma((1,)),
        ],
        compiler_params=pltpu.CompilerParams(
            collective_id=0, has_side_effects=True, vmem_limit_bytes=56 * 1024 * 1024
        ),
        name="sigma",
    )(coefficients.T, integrals, targets, orbital_pairs, phases)
    return sigma_t.T


def solution(mesh):
    in_specs = (P("tile", "wide"), P(), P(), P(), P())
    return jax.shard_map(
        functools.partial(per_device, mesh),
        mesh=mesh,
        in_specs=in_specs,
        out_specs=P("tile", "wide"),
        check_vma=False,
    )
```
